512 devices in a mesh: layer: 16 (over z), col: 32 (over x, y, core).
Axes of the slice: x: 4, y: 4, z: 16, core: 2. Of those that a mesh axis runs over, the one named last changes fastest.
Arguments:
- iterate: float32 [16, 32, 4, 128, 128], P('layer', 'col'), as said below
- residual_in: float32 [16, 32, 4, 128, 128], P('layer', 'col'), as said below
- direction_in: float32 [16, 32, 4, 128, 128], P('layer', 'col'), as said below
- previous_rz: float32 [128], replicated, may hold values from 262144 to 1048576
- local_schur: float32 [16, 32, 512, 512], P('layer', 'col'), as said below
- local_inverse: float32 [16, 32, 512, 512], P('layer', 'col'), as said below
- coarse_inverse: float32 [1024, 1024], P(('layer', 'col')), as said below
- face_included: int32 [16, 32, 4], P('layer', 'col'), may hold values from 0 to 1, as said below
Outputs:
- iterate_out: float32 [16, 32, 4, 128, 128], P('layer', 'col')
- residual_out: float32 [16, 32, 4, 128, 128], P('layer', 'col')
- direction_out: float32 [16, 32, 4, 128, 128], P('layer', 'col')
- rz_out: float32 [128], replicated
The draws below stay inside these ranges and needn't reach their ends.
Inputs may be any that keep to these rules, and one draw needn't show every extreme that they name: `face_included`: 1 where the face is part of the interface; the two subdomains that share a face carry the same flag for it; the lower faces of the first layer and the upper faces of the last layer are 0. `residual_in`: a face shared by two subdomains holds the same values on both. `direction_in`: a face shared by two subdomains holds the same values on both. `iterate`: a face shared by two subdomains holds the same values on both. `coarse_inverse`: symmetric positive definite. `local_schur`: each matrix symmetric positive definite. `local_inverse`: each matrix symmetric positive definite.
All inputs are finite; a program needn't handle non-finite values.
Results may differ from the reference program's by a relative error of at most 0.0002.
Values sent between devices are 32-bit elements; how exact they have to be, the bound alone decides.
A program may use at most 64 MiB of HBM per device.

```python
import math
import jax
import jax.numpy as jnp
from jax import lax

FB = 128
RHS = 128
LAYERS = 16
COLS = 32
NB = 512
NCO = 1024


def expand_faces(owned):
    above = owned[:, :, 0]
    right = owned[:, :, 1]
    return jnp.stack([jnp.roll(above, 1, axis=0), above, jnp.roll(right, 1, axis=1), right], 2)


def symmetric_block(key, lead, size):
    first, second = jax.random.split(key)
    base = jax.random.normal(first, lead + (size, size), jnp.float32)
    spread = 0.45 / math.sqrt(size)
    sym = spread * (base + jnp.swapaxes(base, -1, -2)) / math.sqrt(2.0)
    diagonal = jax.random.uniform(second, lead + (size,), jnp.float32, 1.5, 3.0)
    return sym + jnp.eye(size, dtype=jnp.float32) * diagonal[..., None, :]


def draw_iterate(key, part):
    key = jax.random.fold_in(key, 7)
    shape = (LAYERS, COLS, 2, FB, RHS)
    owned = jax.random.normal(key, shape, jnp.float32)
    return expand_faces(owned)


def draw_residual_in(key, part):
    key = jax.random.fold_in(key, 11)
    shape = (LAYERS, COLS, 2, FB, RHS)
    ramp = 1.0 + 2.0 * jnp.arange(LAYERS, dtype=jnp.float32) / max(LAYERS - 1, 1)
    owned = jax.random.normal(key, shape, jnp.float32)
    return expand_faces(owned * ramp[:, None, None, None, None])


def draw_direction_in(key, part):
    key = jax.random.fold_in(key, 13)
    shape = (LAYERS, COLS, 2, FB, RHS)
    owned = jax.random.normal(key, shape, jnp.float32)
    return expand_faces(owned)


def draw_local_schur(key, part):
    key = jax.random.fold_in(key, 21)
    return symmetric_block(key, (LAYERS, COLS), NB)


def draw_local_inverse(key, part):
    key = jax.random.fold_in(key, 23)
    return symmetric_block(key, (LAYERS, COLS), NB)


def draw_coarse_inverse(key, part):
    key = jax.random.fold_in(key, 29)
    return symmetric_block(key, (), NCO)


def draw_face_included(key, part):
    key = jax.random.fold_in(key, 41)
    flags = jax.random.randint(key, (2, LAYERS, COLS), 0, 4)
    layer_index = jnp.arange(LAYERS, dtype=jnp.int32)[:, None]
    above = jnp.where((flags[0] > 0) & (layer_index < LAYERS - 1), 1, 0).astype(jnp.int32)
    right = jnp.where(flags[1] > 0, 1, 0).astype(jnp.int32)
    return jnp.stack([jnp.roll(above, 1, axis=0), above, jnp.roll(right, 1, axis=1), right], 2).astype(jnp.int32)


def setup_inputs(seed: int = 0) -> dict:
    key_list = jax.random.split(jax.random.key(seed), 9)
    iterate = draw_iterate(jax.random.fold_in(key_list[8], 71), 0)
    residual_in = draw_residual_in(jax.random.fold_in(key_list[8], 71), 0)
    direction_in = draw_direction_in(jax.random.fold_in(key_list[8], 71), 0)
    previous_rz = jnp.clip(jnp.exp(jax.random.uniform(key_list[3], (RHS,), jnp.float32, math.log(262144.0), math.log(1048576))), 262144.0, 1048576)
    local_schur = draw_local_schur(jax.random.fold_in(key_list[8], 71), 0)
    local_inverse = draw_local_inverse(jax.random.fold_in(key_list[8], 71), 0)
    coarse_inverse = draw_coarse_inverse(jax.random.fold_in(key_list[8], 71), 0)
    face_included = draw_face_included(jax.random.fold_in(key_list[8], 71), 0)
    return {"iterate": iterate, "residual_in": residual_in, "direction_in": direction_in, "previous_rz": previous_rz, "local_schur": local_schur, "local_inverse": local_inverse, "coarse_inverse": coarse_inverse, "face_included": face_included}


def free_of_means(field):
    return field - jnp.mean(field, axis=-2, keepdims=True)


def multiply(matrices, field):
    shape = field.shape
    flat = field.reshape(shape[0], shape[1], shape[2] * shape[3], shape[4])
    result = jnp.einsum('lcij,lcjr->lcir', matrices, flat, precision=lax.Precision.HIGHEST)
    return result.reshape(shape)


def assemble(contrib):
    below = contrib[:, :, 0]
    above = contrib[:, :, 1]
    left = contrib[:, :, 2]
    right = contrib[:, :, 3]
    zero_row = jnp.zeros_like(above[:1])
    from_below = jnp.concatenate([zero_row, above[:-1]], 0)
    from_above = jnp.concatenate([below[1:], zero_row], 0)
    from_left = jnp.roll(right, 1, axis=1)
    from_right = jnp.roll(left, -1, axis=1)
    return jnp.stack([below + from_below, above + from_above, left + from_left, right + from_right], axis=2)


def reference(iterate, residual_in, direction_in, previous_rz, local_schur, local_inverse, coarse_inverse, face_included):
    layers, cols = iterate.shape[0], iterate.shape[1]
    columns = iterate.shape[4]
    included = face_included.astype(jnp.float32)[:, :, :, None, None]
    residual = included * residual_in
    previous = included * direction_in
    inner = multiply(local_inverse, free_of_means(0.5 * residual))
    dual = included * free_of_means(inner)
    coarse_res = jnp.stack([residual[:, :, 1], residual[:, :, 3]], 2).mean(axis=3)
    flat = coarse_res.reshape(layers * cols * 2, columns)
    correction = jnp.dot(coarse_inverse, flat, precision=lax.Precision.HIGHEST).reshape(layers, cols, 2, columns)
    owned = jnp.stack([included[:, :, 1, 0], included[:, :, 3, 0]], 2)
    correction = correction * owned
    zero_face = jnp.zeros_like(correction[:, :, 0])
    addon = jnp.stack([zero_face, correction[:, :, 0], zero_face, correction[:, :, 1]], 2)[:, :, :, None, :]
    contrib = 0.5 * dual + addon
    precond = assemble(contrib)
    rz_out = 0.5 * jnp.sum(residual * precond, axis=(0, 1, 2, 3))
    beta = rz_out / previous_rz
    direction = precond + beta * previous
    local_image = included * multiply(local_schur, direction)
    curvature = jnp.sum(direction * local_image, axis=(0, 1, 2, 3))
    alpha = rz_out / curvature
    image = assemble(local_image)
    return iterate + alpha * direction, residual - alpha * image, direction, rz_out
```

```python
import functools
import jax
import jax.numpy as jnp
from jax import lax
from jax.experimental import pallas as pl
from jax.experimental.pallas import tpu as pltpu
from jax.sharding import PartitionSpec as P

MESH = pl.DeviceIdType.MESH
HIGH = lax.Precision.HIGHEST


def mm(a, b):
    return jnp.dot(a, b, precision=HIGH, preferred_element_type=jnp.float32)


def wait_all(ref, count, sem):
    part = ref.at[pl.ds(0, count)]
    pltpu.make_async_copy(part, part, sem).wait()


def kernel(
    layers,
    cols,
    inc_ref,
    prz_ref,
    x_hbm,
    r_hbm,
    q_hbm,
    s_hbm,
    m_hbm,
    c_hbm,
    xo_hbm,
    ro_hbm,
    do_hbm,
    rz_ref,
    xv,
    rv,
    qv,
    sv,
    mv,
    cv,
    outv,
    rhs,
    sqe,
    spv,
    pd,
    hsrc,
    hdst,
    rsend,
    rbuf,
    rflat,
    cbuf_a,
    cbuf_b,
    cfull,
    psend,
    ybuf,
    cpad,
    a1send,
    a1buf,
    a2send,
    a2buf,
    in_sem,
    out_sem,
    send_sem,
    recv_sem,
    hsend_sem,
    hrecv_sem,
):
    fb = xv.shape[0] // 4
    width = 2 * cols
    lanes = rflat.shape[0]
    per = lanes // width
    lay = lax.axis_index("layer")
    col = lax.axis_index("col")
    below = lax.rem(lay + layers - 1, layers)
    above = lax.rem(lay + 1, layers)
    left = lax.rem(col + cols - 1, cols)
    right = lax.rem(col + 1, cols)

    def load(src, dst, i):
        return pltpu.make_async_copy(src, dst, in_sem.at[i])

    loads = [
        load(r_hbm, rv, 0),
        load(c_hbm, cv, 1),
        load(m_hbm, mv, 2),
        load(q_hbm, qv, 3),
        load(s_hbm, sv, 4),
        load(x_hbm, xv, 5),
    ]
    for one in loads:
        one.start()

    barrier = pltpu.get_barrier_semaphore()

    def greet(l, c):
        pl.semaphore_signal(barrier, inc=1, device_id=(l, c), device_id_type=MESH)

    def others(n, me, act):
        def body(k, carry):
            act(lax.rem(me + k, n))
            return carry

        lax.fori_loop(1, n, body, 0)

    def greet_layer(l):
        greet(l, col)
        greet(l, left)

    others(layers, lay, greet_layer)
    others(cols, col, lambda c: greet(lay, c))

    def send(src, dst, i, l, c):
        pltpu.make_async_remote_copy(
            src_ref=src,
            dst_ref=dst,
            send_sem=send_sem.at[i],
            recv_sem=recv_sem.at[i],
            device_id=(l, c),
            device_id_type=MESH,
        ).start()

    def face(f):
        return pl.ds(f * fb, fb)

    def halo(i):
        for f, g, l, c in ((0, 1, below, col), (1, 0, above, col), (2, 3, lay, left), (3, 2, lay, right)):
            pltpu.make_async_remote_copy(
                src_ref=hsrc.at[i, f],
                dst_ref=hdst.at[i, g],
                send_sem=hsend_sem.at[i],
                recv_sem=hrecv_sem.at[i],
                device_id=(l, c),
                device_id_type=MESH,
            ).start()

    def assembled(i, own, f):
        got = hdst[i, f]
        if f == 0:
            got = jnp.where(lay > 0, got, 0.0)
        if f == 1:
            got = jnp.where(lay < layers - 1, got, 0.0)
        return own + got

    inc = [inc_ref[f].astype(jnp.float32) for f in range(4)]

    loads[0].wait()
    means = []
    for f in range(4):
        res = inc[f] * rv[face(f), :]
        rv[face(f), :] = res
        means.append(jnp.mean(res, axis=0, keepdims=True))
    rsend[0:1, :] = means[1]
    rsend[1:2, :] = means[3]
    loads[1].wait()

    pl.semaphore_wait(barrier, 2 * (layers - 1) + cols - 1)

    others(cols, col, lambda c: send(rsend, rbuf.at[col], 0, lay, c))

    def block(l):
        return cv.at[:, pl.ds(pl.multiple_of((l // per) * lanes, lanes), lanes)]

    def send_rows(l):
        send(block(l), cbuf_a.at[lay], 1, l, col)
        send(block(l), cbuf_b.at[lay], 2, l, right)

    others(layers, lay, send_rows)
    send(block(lay), cbuf_b.at[lay], 2, lay, right)
    rbuf[pl.ds(col, 1)] = rsend[...][None]
    cbuf_a[pl.ds(lay, 1)] = cv[:, pl.ds(pl.multiple_of((lay // per) * lanes, lanes), lanes)][None]

    for f in range(4):
        spv[face(f), :] = 0.5 * (rv[face(f), :] - means[f])
    loads[2].wait()
    inner = mm(mv[...], spv[...])
    rz = jnp.zeros_like(means[0])
    for f in range(4):
        part = inner[f * fb : (f + 1) * fb]
        half = 0.5 * (inc[f] * (part - jnp.mean(part, axis=0, keepdims=True)))
        hsrc[0, f] = half
        rz += jnp.sum(rv[face(f), :] * half, axis=0, keepdims=True)
    halo(0)

    loads[3].wait()
    row = lax.broadcasted_iota(jnp.int32, (fb, 128), 1)
    for f in range(4):
        prev = inc[f] * qv[face(f), :]
        qv[face(f), :] = prev
        rhs[face(f), 0:128] = prev
        rhs[face(f), 128:256] = jnp.where(row == f, 1.0, 0.0)
    loads[4].wait()
    sqe[...] = mm(sv[...], rhs[...])
    qq = jnp.zeros_like(rz)
    hq = []
    ke = []
    for f in range(4):
        sq = inc[f] * sqe[face(f), 0:128]
        se = inc[f] * sqe[face(f), 128:256]
        sqe[face(f), 128:256] = se
        hsrc[1, f] = sq
        qq += jnp.sum(qv[face(f), :] * sq, axis=0, keepdims=True)
        hq.append(jnp.sum(sq, axis=0, keepdims=True))
        ke.append(jnp.sum(se, axis=0, keepdims=True))
    halo(1)

    wait_all(cbuf_a, layers - 1, recv_sem.at[1])
    wait_all(cbuf_b, layers, recv_sem.at[2])
    for l in range(layers):
        one = cbuf_a[l]
        two = cbuf_b[l]
        up = (l + 1) % layers
        cfull[4 * up : 4 * up + 1, :] = one[0:1]
        cfull[4 * l + 1 : 4 * l + 2, :] = one[0:1]
        cfull[4 * l + 2 : 4 * l + 3, :] = two[1:2]
        cfull[4 * l + 3 : 4 * l + 4, :] = one[1:2]
    lane = lax.broadcasted_iota(jnp.int32, cfull.shape, 1)
    mine = (lane // width) == lax.rem(lay, per)
    coarse = jnp.where(mine, cfull[...], 0.0)
    wait_all(rbuf, cols - 1, recv_sem.at[0])
    for c in range(cols):
        pair = rbuf[c]
        for k in range(per):
            rflat[k * width + 2 * c : k * width + 2 * c + 2, :] = pair
    part = mm(coarse, rflat[...])
    for l in range(layers):
        psend[l] = part[4 * l : 4 * l + 4]
    others(layers, lay, lambda l: send(psend.at[l], ybuf.at[lay], 3, l, col))
    ybuf[pl.ds(lay, 1)] = psend[pl.ds(lay, 1)]

    wait_all(hdst.at[0], 4, hrecv_sem.at[0])
    for f in range(4):
        pd[face(f), :] = assembled(0, hsrc[0, f], f)
    spv[...] = mm(sv[...], pd[...])
    pp = jnp.zeros_like(rz)
    pq = jnp.zeros_like(rz)
    gp = []
    for f in range(4):
        sp = inc[f] * spv[face(f), :]
        spv[face(f), :] = sp
        here = pd[face(f), :]
        pp += jnp.sum(here * sp, axis=0, keepdims=True)
        pq += jnp.sum(here * hsrc[1, f], axis=0, keepdims=True)
        gp.append(jnp.sum(sp, axis=0, keepdims=True))
    cpad[...] = jnp.zeros_like(cpad)

    wait_all(ybuf, layers - 1, recv_sem.at[3])
    total = jnp.sum(ybuf[...], axis=0)
    cor = [inc[f] * total[f : f + 1] for f in range(4)]
    for f in range(4):
        cpad[f : f + 1, :] = cor[f]
    rz += float(fb) * (means[1] * cor[1] + means[3] * cor[3])
    for f in range(4):
        kc = gp[f] * 2.0
        for g in range(4):
            kc += ke[f][:, g : g + 1] * cor[g]
        pp += cor[f] * kc
        pq += cor[f] * hq[f]
    a1send[0:1, :] = rz
    a1send[1:2, :] = pp
    a1send[2:3, :] = 2.0 * pq
    a1send[3:4, :] = qq
    others(layers, lay, lambda l: send(a1send, a1buf.at[lay], 4, l, col))
    a1buf[pl.ds(lay, 1)] = a1send[...][None]

    change = mm(sqe[:, 128:256], cpad[...])
    for f in range(4):
        hsrc[2, f] = spv[face(f), :] + change[f * fb : (f + 1) * fb]
        pd[face(f), :] = pd[face(f), :] + cor[f]
    halo(2)

    wait_all(a1buf, layers - 1, recv_sem.at[4])
    a2send[...] = jnp.sum(a1buf[...], axis=0)
    others(cols, col, lambda c: send(a2send, a2buf.at[col], 5, lay, c))
    a2buf[pl.ds(col, 1)] = a2send[...][None]
    wait_all(hdst.at[1], 4, hrecv_sem.at[1])
    for f in range(4):
        sqe[face(f), 0:128] = assembled(1, hsrc[1, f], f)
    wait_all(hdst.at[2], 4, hrecv_sem.at[2])
    for f in range(4):
        spv[face(f), :] = assembled(2, hsrc[2, f], f)
    loads[5].wait()

    wait_all(a2buf, cols - 1, recv_sem.at[5])
    sums = jnp.sum(a2buf[...], axis=0)
    rz_all = sums[0:1]
    beta = rz_all / prz_ref[...]
    curvature = sums[1:2] + beta * (sums[2:3] + beta * sums[3:4])
    alpha = rz_all / curvature
    rz_ref[...] = rz_all
    outs = []
    for f in range(4):
        direction = pd[face(f), :] + beta * qv[face(f), :]
        outv[0, f] = direction
        outv[1, f] = xv[face(f), :] + alpha * direction
        image = spv[face(f), :] + beta * sqe[face(f), 0:128]
        outv[2, f] = rv[face(f), :] - alpha * image
    for i, dst in enumerate((do_hbm, xo_hbm, ro_hbm)):
        one = pltpu.make_async_copy(outv.at[i], dst, out_sem.at[i])
        one.start()
        outs.append(one)

    wait_all(rbuf, cols - 1, send_sem.at[0])
    wait_all(cbuf_a, layers - 1, send_sem.at[1])
    wait_all(cbuf_b, layers, send_sem.at[2])
    wait_all(ybuf, layers - 1, send_sem.at[3])
    wait_all(a1buf, layers - 1, send_sem.at[4])
    wait_all(a2buf, cols - 1, send_sem.at[5])
    for i in range(3):
        wait_all(hsrc.at[i], 4, hsend_sem.at[i])
    for one in outs:
        one.wait()


def solution(mesh):
    layers, cols = mesh.shape["layer"], mesh.shape["col"]

    def per_device(
        iterate,
        residual_in,
        direction_in,
        previous_rz,
        local_schur,
        local_inverse,
        coarse_inverse,
        face_included,
    ):
        _, _, _, fb, rhs = iterate.shape
        nb = 4 * fb
        nco = coarse_inverse.shape[1]
        lanes = min(128, nco)
        f32 = jnp.float32
        flat = [v.reshape(nb, rhs) for v in (iterate, residual_in, direction_in)]
        hbm = pl.BlockSpec(memory_space=pltpu.HBM)
        vmem = pl.BlockSpec(memory_space=pltpu.VMEM)
        field = jax.ShapeDtypeStruct((4, fb, rhs), f32)
        vec = pltpu.VMEM((nb, rhs), f32)
        mat = pltpu.VMEM((nb, nb), f32)
        xo, ro, do, rz = pl.pallas_call(
            functools.partial(kernel, layers, cols),
            out_shape=(field, field, field, jax.ShapeDtypeStruct((1, rhs), f32)),
            in_specs=[pl.BlockSpec(memory_space=pltpu.SMEM), vmem] + [hbm] * 6,
            out_specs=(hbm, hbm, hbm, vmem),
            scratch_shapes=[
                vec,
                vec,
                vec,
                mat,
                mat,
                pltpu.VMEM((2, nco), f32),
                pltpu.VMEM((3, 4, fb, rhs), f32),
                pltpu.VMEM((nb, 256), f32),
                pltpu.VMEM((nb, 256), f32),
                vec,
                vec,
                pltpu.VMEM((3, 4, fb, rhs), f32),
                pltpu.VMEM((3, 4, fb, rhs), f32),
                pltpu.VMEM((2, rhs), f32),
                pltpu.VMEM((cols, 2, rhs), f32),
                pltpu.VMEM((lanes, rhs), f32),
                pltpu.VMEM((layers, 2, lanes), f32),
                pltpu.VMEM((layers, 2, lanes), f32),
                pltpu.VMEM((4 * layers, lanes), f32),
                pltpu.VMEM((layers, 4, rhs), f32),
                pltpu.VMEM((layers, 4, rhs), f32),
                pltpu.VMEM((128, rhs), f32),
                pltpu.VMEM((4, rhs), f32),
                pltpu.VMEM((layers, 4, rhs), f32),
                pltpu.VMEM((4, rhs), f32),
                pltpu.VMEM((cols, 4, rhs), f32),
                pltpu.SemaphoreType.DMA((6,)),
                pltpu.SemaphoreType.DMA((3,)),
                pltpu.SemaphoreType.DMA((6,)),
                pltpu.SemaphoreType.DMA((6,)),
                pltpu.SemaphoreType.DMA((3,)),
                pltpu.SemaphoreType.DMA((3,)),
            ],
            compiler_params=pltpu.CompilerParams(
                collective_id=0, has_side_effects=True, vmem_limit_bytes=32 * 1024 * 1024
            ),
        )(
            face_included.reshape(4),
            previous_rz.reshape(1, rhs),
            *flat,
            local_schur.reshape(nb, nb),
            local_inverse.reshape(nb, nb),
            coarse_inverse,
        )
        shape = iterate.shape
        return xo.reshape(shape), ro.reshape(shape), do.reshape(shape), rz.reshape(rhs)

    placed = (
        P("layer", "col", None, None, None),
        P("layer", "col", None, None, None),
        P("layer", "col", None, None, None),
        P(),
        P("layer", "col", None, None),
        P("layer", "col", None, None),
        P(("layer", "col"), None),
        P("layer", "col", None),
    )
    return jax.shard_map(
        per_device,
        mesh=mesh,
        in_specs=placed,
        out_specs=(
            P("layer", "col", None, None, None),
            P("layer", "col", None, None, None),
            P("layer", "col", None, None, None),
            P(),
        ),
        check_vma=False,
    )
```

```python
import functools
import jax
import jax.numpy as jnp
from jax import lax
from jax.experimental import pallas as pl
from jax.experimental.pallas import tpu as pltpu
from jax.sharding import PartitionSpec as P

MESH = pl.DeviceIdType.MESH
HIGH = lax.Precision.HIGHEST
VMEM_LIMIT = 60 * 1024 * 1024


def mm(a, b):
    return jnp.dot(a, b, precision=HIGH, preferred_element_type=jnp.float32)


def wait_all(ref, count, sem):
    part = ref.at[pl.ds(0, count)]
    pltpu.make_async_copy(part, part, sem).wait()


def kernel(
    layers,
    cols,
    inc_ref,
    prz_ref,
    x_hbm,
    r_hbm,
    q_hbm,
    s_hbm,
    m_hbm,
    c_hbm,
    out_ref,
    rz_ref,
    xv,
    rv,
    qv,
    sv,
    mv,
    cv,
    zc,
    csend,
    cbuf_a,
    cbuf_b,
    cfull,
    rhs,
    sqe,
    spv,
    pd,
    hsrc,
    hdst,
    rsend,
    rbuf,
    rflat,
    psend,
    ybuf,
    cpad,
    a1send,
    a1buf,
    a2send,
    a2buf,
    in_sem,
    send_sem,
    recv_sem,
    hsend_sem,
    hrecv_sem,
):
    fb = xv.shape[0] // 4
    width = 2 * cols
    nco = cv.shape[1]
    lanes = min(128, nco)
    npar = lanes // width
    nk = nco // lanes
    lay = lax.axis_index("layer")
    col = lax.axis_index("col")
    below = lax.rem(lay + layers - 1, layers)
    above = lax.rem(lay + 1, layers)
    left = lax.rem(col + cols - 1, cols)
    right = lax.rem(col + 1, cols)

    def load(src, dst, i):
        return pltpu.make_async_copy(src, dst, in_sem.at[i])

    loads = [
        load(r_hbm, rv, 0),
        load(c_hbm, cv, 1),
        load(m_hbm, mv, 2),
        load(q_hbm, qv, 3),
        load(s_hbm, sv, 4),
        load(x_hbm, xv, 5),
    ]
    loads[0].start()

    barrier = pltpu.get_barrier_semaphore()

    def greet(l, c):
        pl.semaphore_signal(barrier, inc=1, device_id=(l, c), device_id_type=MESH)

    def others(n, me, act):
        def body(k, carry):
            act(lax.rem(me + k, n))
            return carry

        lax.fori_loop(1, n, body, 0)

    def greet_col(c):
        greet(lay, c)
        greet(below, c)

    others(layers, lay, lambda l: greet(l, col))
    others(cols, col, greet_col)
    for one in loads[1:]:
        one.start()

    def send(src, dst, i, l, c):
        pltpu.make_async_remote_copy(
            src_ref=src,
            dst_ref=dst,
            send_sem=send_sem.at[i],
            recv_sem=recv_sem.at[i],
            device_id=(l, c),
            device_id_type=MESH,
        ).start()

    def face(f):
        return pl.ds(f * fb, fb)

    def halo(i, axis):
        pairs = ((0, 1, below, col), (1, 0, above, col), (2, 3, lay, left), (3, 2, lay, right))
        for f, g, l, c in pairs[2 * axis : 2 * axis + 2]:
            pltpu.make_async_remote_copy(
                src_ref=hsrc.at[i, f],
                dst_ref=hdst.at[i, g],
                send_sem=hsend_sem.at[i],
                recv_sem=hrecv_sem.at[i],
                device_id=(l, c),
                device_id_type=MESH,
            ).start()

    def assembled(i, own, f):
        got = hdst[i, f]
        if f == 0:
            got = jnp.where(lay > 0, got, 0.0)
        if f == 1:
            got = jnp.where(lay < layers - 1, got, 0.0)
        return own + got

    inc = [inc_ref[f].astype(jnp.float32) for f in range(4)]
    zc[...] = jnp.zeros_like(zc)
    rflat[...] = jnp.zeros_like(rflat)
    cpad[...] = jnp.zeros_like(cpad)

    loads[0].wait()
    means = []
    for f in range(4):
        res = inc[f] * rv[face(f), :]
        rv[face(f), :] = res
        mean = jnp.mean(res, axis=0, keepdims=True)
        means.append(mean)
        spv[face(f), :] = 0.5 * (res - mean)
    rsend[0:1, :] = means[1]
    rsend[1:2, :] = means[3]

    loads[1].wait()
    for k in range(nk):
        for row in range(2):
            zc[row, k : k + 1, :] = cv[row : row + 1, k * lanes : (k + 1) * lanes]
    turned = []
    for row in range(2):
        flip = zc[row].T
        whole = flip[0:width]
        for p in range(1, npar):
            whole += pltpu.roll(flip[p * width : (p + 1) * width], p * (128 // npar), 1)
        turned.append(whole)
    for c in range(cols):
        for row in range(2):
            csend[c, 2 * row : 2 * row + 2, :] = turned[row][2 * c : 2 * c + 2]

    loads[2].wait()
    inner = mm(mv[...], spv[...])
    rz = jnp.zeros_like(means[0])
    for f in range(4):
        part = inner[f * fb : (f + 1) * fb]
        half = 0.5 * (inc[f] * (part - jnp.mean(part, axis=0, keepdims=True)))
        hsrc[0, f] = half
        rz += jnp.sum(rv[face(f), :] * half, axis=0, keepdims=True)

    loads[3].wait()
    lane = lax.broadcasted_iota(jnp.int32, (fb, 128), 1)
    for f in range(4):
        prev = inc[f] * qv[face(f), :]
        qv[face(f), :] = prev
        rhs[face(f), 0:128] = prev
        rhs[face(f), 128:256] = jnp.where(lane == f, 1.0, 0.0)
    loads[4].wait()
    sqe[...] = mm(sv[...], rhs[...])
    qq = jnp.zeros_like(rz)
    hq = []
    ke = []
    for f in range(4):
        sq = inc[f] * sqe[face(f), 0:128]
        se = inc[f] * sqe[face(f), 128:256]
        sqe[face(f), 128:256] = se
        hsrc[1, f] = sq
        qq += jnp.sum(qv[face(f), :] * sq, axis=0, keepdims=True)
        hq.append(jnp.sum(sq, axis=0, keepdims=True))
        ke.append(jnp.sum(se, axis=0, keepdims=True))

    pl.semaphore_wait(barrier, layers - 1 + 2 * (cols - 1))

    others(layers, lay, lambda l: send(rsend, rbuf.at[lay], 0, l, col))

    def send_rows(c):
        send(csend.at[c], cbuf_a.at[col], 1, lay, c)
        send(csend.at[c], cbuf_b.at[col], 2, above, c)

    others(cols, col, send_rows)
    send(csend.at[col], cbuf_b.at[col], 2, above, col)
    halo(0, 0)
    halo(0, 1)
    halo(1, 1)
    rbuf[pl.ds(lay, 1)] = rsend[...][None]
    cbuf_a[pl.ds(col, 1)] = csend[pl.ds(col, 1)]

    wait_all(hdst.at[0], 4, hrecv_sem.at[0])
    for f in range(4):
        pd[face(f), :] = assembled(0, hsrc[0, f], f)
    spv[...] = mm(sv[...], pd[...])
    pp = jnp.zeros_like(rz)
    pq = jnp.zeros_like(rz)
    gp = []
    for f in range(4):
        sp = inc[f] * spv[face(f), :]
        spv[face(f), :] = sp
        here = pd[face(f), :]
        pp += jnp.sum(here * sp, axis=0, keepdims=True)
        pq += jnp.sum(here * hsrc[1, f], axis=0, keepdims=True)
        gp.append(jnp.sum(sp, axis=0, keepdims=True))

    wait_all(cbuf_a, cols - 1, recv_sem.at[1])
    wait_all(cbuf_b, cols, recv_sem.at[2])
    for c in range(cols):
        one = cbuf_a[c]
        two = cbuf_b[c]
        near = (c + 1) % cols
        for g in range(2):
            cfull[g, 4 * c : 4 * c + 1, :] = two[g : g + 1]
            cfull[g, 4 * c + 1 : 4 * c + 2, :] = one[g : g + 1]
            cfull[g, 4 * near + 2 : 4 * near + 3, :] = one[2 + g : 3 + g]
            cfull[g, 4 * c + 3 : 4 * c + 4, :] = one[2 + g : 3 + g]
    coarse = cfull[0] + pltpu.roll(cfull[1], nk, 1)
    wait_all(rbuf, layers - 1, recv_sem.at[0])
    for l in range(layers):
        at = (l % npar) * (128 // npar) + l // npar
        for g in range(2):
            rflat[at + g * nk : at + g * nk + 1, :] = rbuf[l, g : g + 1, :]
    part = mm(coarse, rflat[...])
    for c in range(cols):
        psend[c] = part[4 * c : 4 * c + 4]
    others(cols, col, lambda c: send(psend.at[c], ybuf.at[col], 3, lay, c))
    halo(1, 0)
    ybuf[pl.ds(col, 1)] = psend[pl.ds(col, 1)]

    wait_all(ybuf, cols - 1, recv_sem.at[3])
    total = jnp.sum(ybuf[...], axis=0)
    cor = [inc[f] * total[f : f + 1] for f in range(4)]
    for f in range(4):
        cpad[f : f + 1, :] = cor[f]
    rz += float(fb) * (means[1] * cor[1] + means[3] * cor[3])
    for f in range(4):
        kc = gp[f] * 2.0
        for g in range(4):
            kc += ke[f][:, g : g + 1] * cor[g]
        pp += cor[f] * kc
        pq += cor[f] * hq[f]
    a1send[0:1, :] = rz
    a1send[1:2, :] = pp
    a1send[2:3, :] = 2.0 * pq
    a1send[3:4, :] = qq
    others(layers, lay, lambda l: send(a1send, a1buf.at[lay], 4, l, col))
    a1buf[pl.ds(lay, 1)] = a1send[...][None]

    change = mm(sqe[:, 128:256], cpad[...])
    for f in range(4):
        hsrc[2, f] = spv[face(f), :] + change[f * fb : (f + 1) * fb]
    halo(2, 1)
    halo(2, 0)
    for f in range(4):
        pd[face(f), :] = pd[face(f), :] + cor[f]
    wait_all(hdst.at[1], 4, hrecv_sem.at[1])
    for f in range(4):
        sqe[face(f), 0:128] = assembled(1, hsrc[1, f], f)
    loads[5].wait()

    wait_all(a1buf, layers - 1, recv_sem.at[4])
    a2send[...] = jnp.sum(a1buf[...], axis=0)
    others(cols, col, lambda c: send(a2send, a2buf.at[col], 5, lay, c))
    a2buf[pl.ds(col, 1)] = a2send[...][None]
    wait_all(hdst.at[2], 4, hrecv_sem.at[2])
    for f in range(4):
        spv[face(f), :] = assembled(2, hsrc[2, f], f)
    wait_all(rbuf, layers - 1, send_sem.at[0])
    wait_all(cbuf_a, cols - 1, send_sem.at[1])
    wait_all(cbuf_b, cols, send_sem.at[2])
    wait_all(ybuf, cols - 1, send_sem.at[3])
    wait_all(a1buf, layers - 1, send_sem.at[4])
    for i in range(3):
        wait_all(hsrc.at[i], 4, hsend_sem.at[i])

    wait_all(a2buf, cols - 1, recv_sem.at[5])
    sums = jnp.sum(a2buf[...], axis=0)
    rz_all = sums[0:1]
    beta = rz_all / prz_ref[...]
    curvature = sums[1:2] + beta * (sums[2:3] + beta * sums[3:4])
    alpha = rz_all / curvature
    rz_ref[...] = rz_all
    for f in range(4):
        direction = pd[face(f), :] + beta * qv[face(f), :]
        out_ref[2, f] = direction
        out_ref[0, f] = xv[face(f), :] + alpha * direction
        image = spv[face(f), :] + beta * sqe[face(f), 0:128]
        out_ref[1, f] = rv[face(f), :] - alpha * image
    wait_all(a2buf, cols - 1, send_sem.at[5])


def spread(all_ref, rz_in, x_ref, r_ref, d_ref, rz_ref, sem):
    parts = [(all_ref.at[i], ref) for i, ref in enumerate((x_ref, r_ref, d_ref))]
    parts.append((rz_in, rz_ref))
    copies = [pltpu.make_async_copy(src, dst, sem.at[i]) for i, (src, dst) in enumerate(parts)]
    for one in copies:
        one.start()
    for one in copies:
        one.wait()


def solution(mesh):
    layers, cols = mesh.shape["layer"], mesh.shape["col"]

    def per_device(
        iterate,
        residual_in,
        direction_in,
        previous_rz,
        local_schur,
        local_inverse,
        coarse_inverse,
        face_included,
    ):
        _, _, _, fb, rhs = iterate.shape
        nb = 4 * fb
        nco = coarse_inverse.shape[1]
        lanes = min(128, nco)
        f32 = jnp.float32
        flat = [v.reshape(nb, rhs) for v in (iterate, residual_in, direction_in)]
        hbm = pl.BlockSpec(memory_space=pltpu.HBM)
        vmem = pl.BlockSpec(memory_space=pltpu.VMEM)
        field = jax.ShapeDtypeStruct((4, fb, rhs), f32)
        scalar = jax.ShapeDtypeStruct((1, rhs), f32)
        vec = pltpu.VMEM((nb, rhs), f32)
        mat = pltpu.VMEM((nb, nb), f32)
        wide = pltpu.VMEM((nb, 256), f32)
        every, rz = pl.pallas_call(
            functools.partial(kernel, layers, cols),
            out_shape=(pltpu.VMEM((3, 4, fb, rhs), f32), pltpu.VMEM((1, rhs), f32)),
            in_specs=[pl.BlockSpec(memory_space=pltpu.SMEM), vmem] + [hbm] * 6,
            out_specs=(vmem, vmem),
            scratch_shapes=[
                vec,
                vec,
                vec,
                mat,
                mat,
                pltpu.VMEM((2, nco), f32),
                pltpu.VMEM((2, 128, lanes), f32),
                pltpu.VMEM((cols, 4, 128), f32),
                pltpu.VMEM((cols, 4, 128), f32),
                pltpu.VMEM((cols, 4, 128), f32),
                pltpu.VMEM((2, 4 * cols, 128), f32),
                wide,
                wide,
                vec,
                vec,
                pltpu.VMEM((3, 4, fb, rhs), f32),
                pltpu.VMEM((3, 4, fb, rhs), f32),
                pltpu.VMEM((2, rhs), f32),
                pltpu.VMEM((layers, 2, rhs), f32),
                pltpu.VMEM((128, rhs), f32),
                pltpu.VMEM((cols, 4, rhs), f32),
                pltpu.VMEM((cols, 4, rhs), f32),
                pltpu.VMEM((128, rhs), f32),
                pltpu.VMEM((4, rhs), f32),
                pltpu.VMEM((layers, 4, rhs), f32),
                pltpu.VMEM((4, rhs), f32),
                pltpu.VMEM((cols, 4, rhs), f32),
                pltpu.SemaphoreType.DMA((6,)),
                pltpu.SemaphoreType.DMA((6,)),
                pltpu.SemaphoreType.DMA((6,)),
                pltpu.SemaphoreType.DMA((3,)),
                pltpu.SemaphoreType.DMA((3,)),
            ],
            compiler_params=pltpu.CompilerParams(
                collective_id=0, has_side_effects=True, vmem_limit_bytes=VMEM_LIMIT
            ),
        )(
            face_included.reshape(4),
            previous_rz.reshape(1, rhs),
            *flat,
            local_schur.reshape(nb, nb),
            local_inverse.reshape(nb, nb),
            coarse_inverse,
        )
        xo, ro, do, rz = pl.pallas_call(
            spread,
            out_shape=(field, field, field, scalar),
            in_specs=[vmem] * 2,
            out_specs=(hbm, hbm, hbm, hbm),
            scratch_shapes=[pltpu.SemaphoreType.DMA((4,))],
            compiler_params=pltpu.CompilerParams(vmem_limit_bytes=1024 * 1024),
        )(pltpu.with_memory_space_constraint(every, pltpu.VMEM), pltpu.with_memory_space_constraint(rz, pltpu.VMEM))
        shape = iterate.shape
        return xo.reshape(shape), ro.reshape(shape), do.reshape(shape), rz.reshape(rhs)

    placed = (
        P("layer", "col", None, None, None),
        P("layer", "col", None, None, None),
        P("layer", "col", None, None, None),
        P(),
        P("layer", "col", None, None),
        P("layer", "col", None, None),
        P(("layer", "col"), None),
        P("layer", "col", None),
    )
    return jax.shard_map(
        per_device,
        mesh=mesh,
        in_specs=placed,
        out_specs=(
            P("layer", "col", None, None, None),
            P("layer", "col", None, None, None),
            P("layer", "col", None, None, None),
            P(),
        ),
        check_vma=False,
    )
```

```python
import functools
import jax
import jax.numpy as jnp
from jax import lax
from jax.experimental import pallas as pl
from jax.experimental.pallas import tpu as pltpu
from jax.sharding import PartitionSpec as P

MESH = pl.DeviceIdType.MESH
HIGH = lax.Precision.HIGHEST
VMEM_LIMIT = 60 * 1024 * 1024


def mm(a, b):
    return jnp.dot(a, b, precision=HIGH, preferred_element_type=jnp.float32)


def wait_all(ref, count, sem):
    part = ref.at[pl.ds(0, count)]
    pltpu.make_async_copy(part, part, sem).wait()


def kernel(
    layers,
    cols,
    inc_ref,
    prz_ref,
    x_hbm,
    r_hbm,
    q_hbm,
    s_hbm,
    m_hbm,
    c_hbm,
    out_ref,
    rz_ref,
    xv,
    rv,
    qv,
    sv,
    mv,
    cv,
    rhs,
    sqe,
    spv,
    pd,
    hsrc,
    hdst,
    rsend,
    rbuf,
    cbuf,
    zmat,
    ct,
    turned,
    rall,
    ksend,
    kbuf,
    csend,
    crecv,
    cpad,
    a2send,
    a2buf,
    ssend,
    srecv,
    in_sem,
    send_sem,
    recv_sem,
    hsend_sem,
    hrecv_sem,
):
    fb = xv.shape[0] // 4
    width = 2 * cols
    nco = cv.shape[1]
    lanes = min(128, nco)
    lay = lax.axis_index("layer")
    col = lax.axis_index("col")
    below = lax.rem(lay + layers - 1, layers)
    above = lax.rem(lay + 1, layers)
    left = lax.rem(col + cols - 1, cols)
    right = lax.rem(col + 1, cols)
    center = lay == 0
    outer = lay != 0

    def load(src, dst, i):
        return pltpu.make_async_copy(src, dst, in_sem.at[i])

    loads = [
        load(r_hbm, rv, 0),
        load(c_hbm, cv, 1),
        load(m_hbm, mv, 2),
        load(q_hbm, qv, 3),
        load(s_hbm, sv, 4),
        load(x_hbm, xv, 5),
    ]
    loads[0].start()

    barrier = pltpu.get_barrier_semaphore()

    def greet(l, c):
        pl.semaphore_signal(barrier, inc=1, device_id=(l, c), device_id_type=MESH)

    def others(n, me, act):
        def body(k, carry):
            act(lax.rem(me + k, n))
            return carry

        lax.fori_loop(1, n, body, 0)

    def send(src, dst, i, l, c):
        pltpu.make_async_remote_copy(
            src_ref=src,
            dst_ref=dst,
            send_sem=send_sem.at[i],
            recv_sem=recv_sem.at[i],
            device_id=(l, c),
            device_id_type=MESH,
        ).start()

    greet(below, col)
    greet(above, col)
    greet(lay, left)
    greet(lay, right)

    @pl.when(outer)
    def _():
        greet(0, col)

    for one in loads[1:]:
        one.start()

    @pl.when(center)
    def _():
        others(layers, lay, lambda l: greet(l, col))
        others(cols, col, lambda c: greet(lay, c))

    def face(f):
        return pl.ds(f * fb, fb)

    def halo(i):
        pairs = ((0, 1, below, col), (1, 0, above, col), (2, 3, lay, left), (3, 2, lay, right))
        for f, g, l, c in pairs:
            pltpu.make_async_remote_copy(
                src_ref=hsrc.at[i, f],
                dst_ref=hdst.at[i, g],
                send_sem=hsend_sem.at[i],
                recv_sem=hrecv_sem.at[i],
                device_id=(l, c),
                device_id_type=MESH,
            ).start()

    def assembled(i, own, f):
        got = hdst[i, f]
        if f == 0:
            got = jnp.where(lay > 0, got, 0.0)
        if f == 1:
            got = jnp.where(lay < layers - 1, got, 0.0)
        return own + got

    inc = [inc_ref[f].astype(jnp.float32) for f in range(4)]
    cpad[...] = jnp.zeros_like(cpad)

    loads[0].wait()
    means = []
    for f in range(4):
        res = inc[f] * rv[face(f), :]
        rv[face(f), :] = res
        mean = jnp.mean(res, axis=0, keepdims=True)
        means.append(mean)
        spv[face(f), :] = 0.5 * (res - mean)
    rsend[0:1, :] = means[1]
    rsend[1:2, :] = means[3]
    loads[1].wait()

    @pl.when(center)
    def _():
        zmat[3 * layers :, :] = jnp.zeros((zmat.shape[0] - 3 * layers, nco), jnp.float32)
        rbuf[0] = rsend[...]
        cbuf[0] = cv[...]
        pl.semaphore_wait(barrier, 4 + layers - 1 + cols - 1)

    @pl.when(outer)
    def _():
        pl.semaphore_wait(barrier, 5)
        send(rsend, rbuf.at[lay], 0, 0, col)
        send(cv, cbuf.at[lay], 1, 0, col)

    loads[2].wait()
    inner = mm(mv[...], spv[...])
    rz = jnp.zeros_like(means[0])
    for f in range(4):
        part = inner[f * fb : (f + 1) * fb]
        half = 0.5 * (inc[f] * (part - jnp.mean(part, axis=0, keepdims=True)))
        hsrc[0, f] = half
        rz += jnp.sum(rv[face(f), :] * half, axis=0, keepdims=True)
    halo(0)
    ksend[8:9, :] = rz

    loads[3].wait()
    lane = lax.broadcasted_iota(jnp.int32, (fb, 128), 1)
    for f in range(4):
        prev = inc[f] * qv[face(f), :]
        qv[face(f), :] = prev
        rhs[face(f), 0:128] = prev
        rhs[face(f), 128:256] = jnp.where(lane == f, inc[f], 0.0)
    loads[4].wait()
    sqe[...] = mm(sv[...], rhs[...])
    qq = jnp.zeros_like(rz)
    for f in range(4):
        sq = inc[f] * sqe[face(f), 0:128]
        se = inc[f] * sqe[face(f), 128:256]
        sqe[face(f), 128:256] = se
        hsrc[1, f] = sq
        qq += jnp.sum(qv[face(f), :] * sq, axis=0, keepdims=True)
        ksend[4 + f : 5 + f, :] = 2.0 * jnp.sum(sq, axis=0, keepdims=True)
        ksend[12 + f : 13 + f, :] = jnp.sum(se, axis=0, keepdims=True)
    halo(1)
    ksend[11:12, :] = qq

    @pl.when(center)
    def _():
        wait_all(rbuf, layers - 1, recv_sem.at[0])
        for l in range(layers):
            for g in range(2):
                rall[col, g * layers + l : g * layers + l + 1, :] = rbuf[l, g : g + 1, :]
        others(cols, col, lambda c: send(rall.at[col], rall.at[col], 2, 0, c))
        wait_all(cbuf, layers - 1, recv_sem.at[1])
        for l in range(layers):
            for g in range(2):
                zmat[g * layers + l : g * layers + l + 1, :] = cbuf[l, g : g + 1, :]
        mid = zmat.at[pl.ds(layers, layers)]
        send(mid, zmat.at[pl.ds(2 * layers, layers)], 7, 0, right)

    wait_all(hdst.at[0], 4, hrecv_sem.at[0])
    for f in range(4):
        pd[face(f), :] = assembled(0, hsrc[0, f], f)
    spv[...] = mm(sv[...], pd[...])
    pp = jnp.zeros_like(rz)
    pq = jnp.zeros_like(rz)
    for f in range(4):
        sp = inc[f] * spv[face(f), :]
        spv[face(f), :] = sp
        here = pd[face(f), :]
        pp += jnp.sum(here * sp, axis=0, keepdims=True)
        pq += jnp.sum(here * hsrc[1, f], axis=0, keepdims=True)
        ksend[f : f + 1, :] = 2.0 * jnp.sum(sp, axis=0, keepdims=True)
    ksend[9:10, :] = pp
    ksend[10:11, :] = 2.0 * pq

    @pl.when(outer)
    def _():
        send(ksend, kbuf.at[lay], 3, 0, col)

    @pl.when(center)
    def _():
        wait_all(zmat, layers, recv_sem.at[7])
        wait_all(zmat, layers, send_sem.at[7])
        for j in range(nco // lanes):
            ct[j * lanes : (j + 1) * lanes, :] = zmat[:, j * lanes : (j + 1) * lanes].T
        for c in range(cols):
            for g in range(2):
                at = (2 * c + g) * layers
                turned[at : at + layers, :] = ct[pl.ds(2 * c + g, layers, stride=width), :]
        for j in range(nco // lanes):
            zmat[:, j * lanes : (j + 1) * lanes] = turned[j * lanes : (j + 1) * lanes, :].T

    wait_all(hdst.at[1], 4, hrecv_sem.at[1])
    for f in range(4):
        sqe[face(f), 0:128] = assembled(1, hsrc[1, f], f)
    loads[5].wait()

    @pl.when(center)
    def _():
        kbuf[0] = ksend[...]
        wait_all(rall, cols - 1, recv_sem.at[2])
        total = mm(zmat[0 : 3 * layers, :], rall[...].reshape(nco, rall.shape[2]))
        for l in range(layers):
            low = (l + layers - 1) % layers
            csend[l, 0:1, :] = total[low : low + 1]
            csend[l, 1:2, :] = total[l : l + 1]
            csend[l, 2:3, :] = total[2 * layers + l : 2 * layers + l + 1]
            csend[l, 3:4, :] = total[layers + l : layers + l + 1]
        others(layers, lay, lambda l: send(csend.at[l], crecv, 4, l, col))
        wait_all(kbuf, layers - 1, recv_sem.at[3])
        base = jnp.zeros_like(a2send)
        quad = jnp.zeros_like(a2send)
        cross = jnp.zeros_like(a2send)
        work = jnp.zeros((1, a2send.shape[1]), jnp.float32)
        for l in range(layers):
            cor = csend[l]
            mixed = kbuf[l, 0:4, :]
            block = kbuf[l, 12:16, :]
            for g in range(4):
                mixed += block[:, g : g + 1] * cor[g : g + 1]
            quad += cor * mixed
            cross += cor * kbuf[l, 4:8, :]
            base += kbuf[l, 8:12, :]
            work += rbuf[l, 0:1, :] * cor[1:2] + rbuf[l, 1:2, :] * cor[3:4]
        a2send[0:1, :] = base[0:1] + float(fb) * work
        a2send[1:2, :] = base[1:2] + jnp.sum(quad, axis=0, keepdims=True)
        a2send[2:3, :] = base[2:3] + jnp.sum(cross, axis=0, keepdims=True)
        a2send[3:4, :] = base[3:4]
        others(cols, col, lambda c: send(a2send, a2buf.at[col], 5, lay, c))
        a2buf[pl.ds(col, 1)] = a2send[...][None]
        crecv[...] = csend[0]

    @pl.when(outer)
    def _():
        wait_all(crecv, 4, recv_sem.at[4])

    cor = [inc[f] * crecv[f : f + 1, :] for f in range(4)]
    for f in range(4):
        cpad[f : f + 1, :] = cor[f]
    change = mm(sqe[:, 128:256], cpad[...])
    for f in range(4):
        hsrc[2, f] = spv[face(f), :] + change[f * fb : (f + 1) * fb]
    halo(2)
    for f in range(4):
        pd[face(f), :] = pd[face(f), :] + cor[f]

    @pl.when(center)
    def _():
        wait_all(a2buf, cols - 1, recv_sem.at[5])
        ssend[...] = jnp.sum(a2buf[...], axis=0)
        others(layers, lay, lambda l: send(ssend, srecv, 6, l, col))
        srecv[...] = ssend[...]

    wait_all(hdst.at[2], 4, hrecv_sem.at[2])
    for f in range(4):
        spv[face(f), :] = assembled(2, hsrc[2, f], f)

    @pl.when(outer)
    def _():
        wait_all(srecv, 4, recv_sem.at[6])

    sums = srecv[...]
    rz_all = sums[0:1]
    beta = rz_all / prz_ref[...]
    curvature = sums[1:2] + beta * (sums[2:3] + beta * sums[3:4])
    alpha = rz_all / curvature
    rz_ref[...] = rz_all
    for f in range(4):
        direction = pd[face(f), :] + beta * qv[face(f), :]
        out_ref[2, f] = direction
        out_ref[0, f] = xv[face(f), :] + alpha * direction
        image = spv[face(f), :] + beta * sqe[face(f), 0:128]
        out_ref[1, f] = rv[face(f), :] - alpha * image

    for i in range(3):
        wait_all(hsrc.at[i], 4, hsend_sem.at[i])

    @pl.when(center)
    def _():
        wait_all(rall, cols - 1, send_sem.at[2])
        wait_all(csend, layers - 1, send_sem.at[4])
        wait_all(a2buf, cols - 1, send_sem.at[5])
        wait_all(csend, layers - 1, send_sem.at[6])

    @pl.when(outer)
    def _():
        wait_all(rsend, 2, send_sem.at[0])
        wait_all(cv, 2, send_sem.at[1])
        wait_all(ksend, 16, send_sem.at[3])


def spread(all_ref, rz_in, x_ref, r_ref, d_ref, rz_ref, sem):
    parts = [(all_ref.at[i], ref) for i, ref in enumerate((x_ref, r_ref, d_ref))]
    parts.append((rz_in, rz_ref))
    copies = [pltpu.make_async_copy(src, dst, sem.at[i]) for i, (src, dst) in enumerate(parts)]
    for one in copies:
        one.start()
    for one in copies:
        one.wait()


def solution(mesh):
    layers, cols = mesh.shape["layer"], mesh.shape["col"]

    def per_device(
        iterate,
        residual_in,
        direction_in,
        previous_rz,
        local_schur,
        local_inverse,
        coarse_inverse,
        face_included,
    ):
        _, _, _, fb, rhs = iterate.shape
        nb = 4 * fb
        nco = coarse_inverse.shape[1]
        f32 = jnp.float32
        flat = [v.reshape(nb, rhs) for v in (iterate, residual_in, direction_in)]
        hbm = pl.BlockSpec(memory_space=pltpu.HBM)
        vmem = pl.BlockSpec(memory_space=pltpu.VMEM)
        field = jax.ShapeDtypeStruct((4, fb, rhs), f32)
        scalar = jax.ShapeDtypeStruct((1, rhs), f32)
        vec = pltpu.VMEM((nb, rhs), f32)
        mat = pltpu.VMEM((nb, nb), f32)
        wide = pltpu.VMEM((nb, 256), f32)
        every, rz = pl.pallas_call(
            functools.partial(kernel, layers, cols),
            out_shape=(pltpu.VMEM((3, 4, fb, rhs), f32), pltpu.VMEM((1, rhs), f32)),
            in_specs=[pl.BlockSpec(memory_space=pltpu.SMEM), vmem] + [hbm] * 6,
            out_specs=(vmem, vmem),
            scratch_shapes=[
                vec,
                vec,
                vec,
                mat,
                mat,
                pltpu.VMEM((2, nco), f32),
                wide,
                wide,
                vec,
                vec,
                pltpu.VMEM((3, 4, fb, rhs), f32),
                pltpu.VMEM((3, 4, fb, rhs), f32),
                pltpu.VMEM((2, rhs), f32),
                pltpu.VMEM((layers, 2, rhs), f32),
                pltpu.VMEM((layers, 2, nco), f32),
                pltpu.VMEM((128, nco), f32),
                pltpu.VMEM((nco, 128), f32),
                pltpu.VMEM((nco, 128), f32),
                pltpu.VMEM((cols, 2 * layers, rhs), f32),
                pltpu.VMEM((16, rhs), f32),
                pltpu.VMEM((layers, 16, rhs), f32),
                pltpu.VMEM((layers, 4, rhs), f32),
                pltpu.VMEM((4, rhs), f32),
                pltpu.VMEM((128, rhs), f32),
                pltpu.VMEM((4, rhs), f32),
                pltpu.VMEM((cols, 4, rhs), f32),
                pltpu.VMEM((4, rhs), f32),
                pltpu.VMEM((4, rhs), f32),
                pltpu.SemaphoreType.DMA((6,)),
                pltpu.SemaphoreType.DMA((8,)),
                pltpu.SemaphoreType.DMA((8,)),
                pltpu.SemaphoreType.DMA((3,)),
                pltpu.SemaphoreType.DMA((3,)),
            ],
            compiler_params=pltpu.CompilerParams(
                collective_id=0, has_side_effects=True, vmem_limit_bytes=VMEM_LIMIT
            ),
        )(
            face_included.reshape(4),
            previous_rz.reshape(1, rhs),
            *flat,
            local_schur.reshape(nb, nb),
            local_inverse.reshape(nb, nb),
            coarse_inverse,
        )
        xo, ro, do, rz = pl.pallas_call(
            spread,
            out_shape=(field, field, field, scalar),
            in_specs=[vmem] * 2,
            out_specs=(hbm, hbm, hbm, hbm),
            scratch_shapes=[pltpu.SemaphoreType.DMA((4,))],
            compiler_params=pltpu.CompilerParams(vmem_limit_bytes=1024 * 1024),
        )(pltpu.with_memory_space_constraint(every, pltpu.VMEM), pltpu.with_memory_space_constraint(rz, pltpu.VMEM))
        shape = iterate.shape
        return xo.reshape(shape), ro.reshape(shape), do.reshape(shape), rz.reshape(rhs)

    placed = (
        P("layer", "col", None, None, None),
        P("layer", "col", None, None, None),
        P("layer", "col", None, None, None),
        P(),
        P("layer", "col", None, None),
        P("layer", "col", None, None),
        P(("layer", "col"), None),
        P("layer", "col", None),
    )
    return jax.shard_map(
        per_device,
        mesh=mesh,
        in_specs=placed,
        out_specs=(
            P("layer", "col", None, None, None),
            P("layer", "col", None, None, None),
            P("layer", "col", None, None, None),
            P(),
        ),
        check_vma=False,
    )
```

```python
import functools
import jax
import jax.numpy as jnp
from jax import lax
from jax.experimental import pallas as pl
from jax.experimental.pallas import tpu as pltpu
from jax.sharding import PartitionSpec as P

MESH = pl.DeviceIdType.MESH
HIGH = lax.Precision.HIGHEST
VMEM_LIMIT = 60 * 1024 * 1024


def mm(a, b):
    return jnp.dot(a, b, precision=HIGH, preferred_element_type=jnp.float32)


def wait_all(ref, count, sem):
    part = ref.at[pl.ds(0, count)]
    pltpu.make_async_copy(part, part, sem).wait()


def kernel(
    layers,
    cols,
    inc_ref,
    prz_ref,
    x_hbm,
    r_hbm,
    q_hbm,
    s_hbm,
    m_hbm,
    c_hbm,
    out_ref,
    rz_ref,
    xv,
    rv,
    qv,
    sv,
    mv,
    cv,
    rhs,
    sqe,
    spv,
    pd,
    hsrc,
    hdst,
    rsend,
    rbuf,
    cbuf,
    zmat,
    ct,
    turned,
    rall,
    rlate,
    ksend,
    kbuf,
    csend,
    crecv,
    cpad,
    a2send,
    a2buf,
    ssend,
    srecv,
    in_sem,
    send_sem,
    recv_sem,
    hsend_sem,
    hrecv_sem,
):
    fb = xv.shape[0] // 4
    width = 2 * cols
    nco = cv.shape[1]
    lanes = min(128, nco)
    lay = lax.axis_index("layer")
    col = lax.axis_index("col")
    below = lax.rem(lay + layers - 1, layers)
    above = lax.rem(lay + 1, layers)
    left = lax.rem(col + cols - 1, cols)
    right = lax.rem(col + 1, cols)
    center = lay == 0
    outer = lay != 0
    top = lay == layers - 1
    inside = outer & (lay != layers - 1)
    first, last = max(1, layers // 2 - 1), min(layers, layers // 2 + 3)
    late = list(range(first, last))
    early = [l for l in range(layers) if l not in late]
    far = (lay >= first) & (lay < last)

    def face(f):
        return pl.ds(f * fb, fb)

    def load(src, dst, i):
        return pltpu.make_async_copy(src, dst, in_sem.at[i])

    loads = [
        load(r_hbm.at[1], rv.at[face(1), :], 0),
        load(c_hbm, cv, 1),
        load(m_hbm, mv, 2),
        load(q_hbm, qv, 3),
        load(s_hbm, sv, 4),
        load(x_hbm, xv, 5),
        load(r_hbm.at[3], rv.at[face(3), :], 6),
        load(r_hbm.at[0], rv.at[face(0), :], 7),
        load(r_hbm.at[2], rv.at[face(2), :], 8),
    ]
    loads[0].start()
    loads[6].start()

    barrier = pltpu.get_barrier_semaphore()

    def greet(l, c):
        pl.semaphore_signal(barrier, inc=1, device_id=(l, c), device_id_type=MESH)

    def others(n, me, act):
        def body(k, carry):
            act(lax.rem(me + k, n))
            return carry

        lax.fori_loop(1, n, body, 0)

    def send(src, dst, i, l, c):
        pltpu.make_async_remote_copy(
            src_ref=src,
            dst_ref=dst,
            send_sem=send_sem.at[i],
            recv_sem=recv_sem.at[i],
            device_id=(l, c),
            device_id_type=MESH,
        ).start()

    greet(lay, left)
    greet(lay, right)
    pl.when(outer)(lambda: greet(below, col))
    pl.when(jnp.logical_not(top))(lambda: greet(above, col))
    for i in (7, 8, 1, 2, 3, 4, 5):
        loads[i].start()

    @pl.when(center)
    def _():
        others(layers, lay, lambda l: greet(l, col))
        others(cols, col, lambda c: greet(lay, c))

    def halo(i):
        def one(f, g, l, c):
            pltpu.make_async_remote_copy(
                src_ref=hsrc.at[i, f],
                dst_ref=hdst.at[i, g],
                send_sem=hsend_sem.at[i],
                recv_sem=hrecv_sem.at[i],
                device_id=(l, c),
                device_id_type=MESH,
            ).start()

        pl.when(outer)(lambda: one(0, 1, below, col))
        pl.when(jnp.logical_not(top))(lambda: one(1, 0, above, col))
        one(2, 3, lay, left)
        one(3, 2, lay, right)

    def halo_wait(i, sem):
        pl.when(inside)(lambda: wait_all(hdst.at[i], 4, sem.at[i]))
        pl.when(jnp.logical_not(inside))(lambda: wait_all(hdst.at[i], 3, sem.at[i]))

    def assembled(i, own, f):
        got = hdst[i, f]
        if f == 0:
            got = jnp.where(lay > 0, got, 0.0)
        if f == 1:
            got = jnp.where(lay < layers - 1, got, 0.0)
        return own + got

    inc = [inc_ref[f].astype(jnp.float32) for f in range(4)]
    cpad[...] = jnp.zeros_like(cpad)

    means = {}

    def average(f, i):
        loads[i].wait()
        res = inc[f] * rv[face(f), :]
        rv[face(f), :] = res
        means[f] = jnp.mean(res, axis=0, keepdims=True)
        spv[face(f), :] = 0.5 * (res - means[f])

    average(1, 0)
    average(3, 6)
    rsend[0:1, :] = means[1]
    rsend[1:2, :] = means[3]

    @pl.when(center)
    def _():
        zmat[3 * layers :, :] = jnp.zeros((zmat.shape[0] - 3 * layers, nco), jnp.float32)
        rbuf[0] = rsend[...]
        loads[1].wait()
        cbuf[0] = cv[...]
    @pl.when(outer)
    def _():
        pl.when(top)(lambda: pl.semaphore_wait(barrier, 4))
        pl.when(inside)(lambda: pl.semaphore_wait(barrier, 5))

        @pl.when(far)
        def _():
            send(rsend, rbuf.at[lay], 8, 0, col)

        @pl.when(jnp.logical_not(far))
        def _():
            send(rsend, rbuf.at[lay], 0, 0, col)

        loads[1].wait()
        send(cv, cbuf.at[lay], 1, 0, col)

    average(0, 7)
    average(2, 8)
    loads[2].wait()
    inner = mm(mv[...], spv[...])
    rz = jnp.zeros_like(means[0])
    for f in range(4):
        part = inner[f * fb : (f + 1) * fb]
        half = 0.5 * (inc[f] * (part - jnp.mean(part, axis=0, keepdims=True)))
        hsrc[0, f] = half
        rz += jnp.sum(rv[face(f), :] * half, axis=0, keepdims=True)
    pl.when(outer)(lambda: halo(0))
    ksend[8:9, :] = rz

    loads[3].wait()
    lane = lax.broadcasted_iota(jnp.int32, (fb, 128), 1)
    for f in range(4):
        prev = inc[f] * qv[face(f), :]
        qv[face(f), :] = prev
        rhs[face(f), 0:128] = prev
        rhs[face(f), 128:256] = jnp.where(lane == f, inc[f], 0.0)
    loads[4].wait()
    sqe[...] = mm(sv[...], rhs[...])
    qq = jnp.zeros_like(rz)
    for f in range(4):
        sq = inc[f] * sqe[face(f), 0:128]
        se = inc[f] * sqe[face(f), 128:256]
        sqe[face(f), 128:256] = se
        hsrc[1, f] = sq
        qq += jnp.sum(qv[face(f), :] * sq, axis=0, keepdims=True)
        ksend[4 + f : 5 + f, :] = 2.0 * jnp.sum(sq, axis=0, keepdims=True)
        ksend[12 + f : 13 + f, :] = jnp.sum(se, axis=0, keepdims=True)
    pl.when(outer)(lambda: halo(1))
    ksend[11:12, :] = qq

    @pl.when(center)
    def _():
        pl.semaphore_wait(barrier, 3 + cols - 1)
        halo(0)
        halo(1)
        wait_all(rbuf, len(early) - 1, recv_sem.at[0])
        for i, l in enumerate(early):
            for g in range(2):
                at = g * len(early) + i
                rall[col, at : at + 1, :] = rbuf[l, g : g + 1, :]
        others(cols, col, lambda c: send(rall.at[col], rall.at[col], 2, 0, c))
        wait_all(rbuf, len(late), recv_sem.at[8])
        for i, l in enumerate(late):
            for g in range(2):
                at = g * len(late) + i
                rlate[col, at : at + 1, :] = rbuf[l, g : g + 1, :]
        others(cols, col, lambda c: send(rlate.at[col], rlate.at[col], 9, 0, c))
        wait_all(cbuf, layers - 1, recv_sem.at[1])
        for l in range(layers):
            for g in range(2):
                zmat[g * layers + l : g * layers + l + 1, :] = cbuf[l, g : g + 1, :]
        mid = zmat.at[pl.ds(layers, layers)]
        send(mid, zmat.at[pl.ds(2 * layers, layers)], 7, 0, right)

    halo_wait(0, hrecv_sem)
    for f in range(4):
        pd[face(f), :] = assembled(0, hsrc[0, f], f)
    spv[...] = mm(sv[...], pd[...])
    pp = jnp.zeros_like(rz)
    pq = jnp.zeros_like(rz)
    for f in range(4):
        sp = inc[f] * spv[face(f), :]
        spv[face(f), :] = sp
        here = pd[face(f), :]
        pp += jnp.sum(here * sp, axis=0, keepdims=True)
        pq += jnp.sum(here * hsrc[1, f], axis=0, keepdims=True)
        ksend[f : f + 1, :] = 2.0 * jnp.sum(sp, axis=0, keepdims=True)
    ksend[9:10, :] = pp
    ksend[10:11, :] = 2.0 * pq

    @pl.when(outer)
    def _():
        send(ksend, kbuf.at[lay], 3, 0, col)

    @pl.when(center)
    def _():
        wait_all(zmat, layers, recv_sem.at[7])
        wait_all(zmat, layers, send_sem.at[7])
        for j in range(nco // lanes):
            ct[j * lanes : (j + 1) * lanes, :] = zmat[:, j * lanes : (j + 1) * lanes].T
        for c in range(cols):
            for g in range(2):
                at = (2 * c + g) * len(early)
                end = 2 * cols * len(early) + (2 * c + g) * len(late)
                for src, dst, n in (
                    (0, at, first),
                    (last, at + first, layers - last),
                    (first, end, len(late)),
                ):
                    if n:
                        rows = ct[pl.ds(src * width + 2 * c + g, n, stride=width), :]
                        turned[dst : dst + n, :] = rows
        for j in range(nco // lanes):
            zmat[:, j * lanes : (j + 1) * lanes] = turned[j * lanes : (j + 1) * lanes, :].T

    halo_wait(1, hrecv_sem)
    for f in range(4):
        sqe[face(f), 0:128] = assembled(1, hsrc[1, f], f)
    loads[5].wait()

    @pl.when(center)
    def _():
        kbuf[0] = ksend[...]
        wait_all(rall, cols - 1, recv_sem.at[2])
        cut = 2 * cols * len(early)
        total = mm(zmat[0 : 3 * layers, 0:cut], rall[...].reshape(cut, rall.shape[2]))
        wait_all(rlate, cols - 1, recv_sem.at[9])
        rest = rlate[...].reshape(nco - cut, rall.shape[2])
        total += mm(zmat[0 : 3 * layers, cut:nco], rest)
        for l in range(layers):
            low = (l + layers - 1) % layers
            csend[l, 0:1, :] = total[low : low + 1]
            csend[l, 1:2, :] = total[l : l + 1]
            csend[l, 2:3, :] = total[2 * layers + l : 2 * layers + l + 1]
            csend[l, 3:4, :] = total[layers + l : layers + l + 1]
        others(layers, lay, lambda l: send(csend.at[l], crecv, 4, l, col))
        wait_all(kbuf, layers - 1, recv_sem.at[3])
        base = jnp.zeros_like(a2send)
        quad = jnp.zeros_like(a2send)
        cross = jnp.zeros_like(a2send)
        work = jnp.zeros((1, a2send.shape[1]), jnp.float32)
        for l in range(layers):
            cor = csend[l]
            mixed = kbuf[l, 0:4, :]
            block = kbuf[l, 12:16, :]
            for g in range(4):
                mixed += block[:, g : g + 1] * cor[g : g + 1]
            quad += cor * mixed
            cross += cor * kbuf[l, 4:8, :]
            base += kbuf[l, 8:12, :]
            work += rbuf[l, 0:1, :] * cor[1:2] + rbuf[l, 1:2, :] * cor[3:4]
        a2send[0:1, :] = base[0:1] + float(fb) * work
        a2send[1:2, :] = base[1:2] + jnp.sum(quad, axis=0, keepdims=True)
        a2send[2:3, :] = base[2:3] + jnp.sum(cross, axis=0, keepdims=True)
        a2send[3:4, :] = base[3:4]
        others(cols, col, lambda c: send(a2send, a2buf.at[col], 5, lay, c))
        a2buf[pl.ds(col, 1)] = a2send[...][None]
        crecv[...] = csend[0]

    @pl.when(outer)
    def _():
        wait_all(crecv, 4, recv_sem.at[4])

    cor = [inc[f] * crecv[f : f + 1, :] for f in range(4)]
    for f in range(4):
        cpad[f : f + 1, :] = cor[f]
    change = mm(sqe[:, 128:256], cpad[...])
    for f in range(4):
        hsrc[2, f] = spv[face(f), :] + change[f * fb : (f + 1) * fb]
    halo(2)
    for f in range(4):
        pd[face(f), :] = pd[face(f), :] + cor[f]

    @pl.when(center)
    def _():
        wait_all(a2buf, cols - 1, recv_sem.at[5])
        ssend[...] = jnp.sum(a2buf[...], axis=0)
        others(layers, lay, lambda l: send(ssend, srecv, 6, l, col))
        srecv[...] = ssend[...]

    halo_wait(2, hrecv_sem)
    for f in range(4):
        spv[face(f), :] = assembled(2, hsrc[2, f], f)

    @pl.when(outer)
    def _():
        wait_all(srecv, 4, recv_sem.at[6])

    sums = srecv[...]
    rz_all = sums[0:1]
    beta = rz_all / prz_ref[...]
    curvature = sums[1:2] + beta * (sums[2:3] + beta * sums[3:4])
    alpha = rz_all / curvature
    rz_ref[...] = rz_all
    for f in range(4):
        direction = pd[face(f), :] + beta * qv[face(f), :]
        out_ref[2, f] = direction
        out_ref[0, f] = xv[face(f), :] + alpha * direction
        image = spv[face(f), :] + beta * sqe[face(f), 0:128]
        out_ref[1, f] = rv[face(f), :] - alpha * image

    for i in range(3):
        halo_wait(i, hsend_sem)

    @pl.when(center)
    def _():
        wait_all(rall, cols - 1, send_sem.at[2])
        wait_all(rlate, cols - 1, send_sem.at[9])
        wait_all(csend, layers - 1, send_sem.at[4])
        wait_all(a2buf, cols - 1, send_sem.at[5])
        wait_all(csend, layers - 1, send_sem.at[6])

    @pl.when(outer)
    def _():
        pl.when(far)(lambda: wait_all(rsend, 2, send_sem.at[8]))
        pl.when(jnp.logical_not(far))(lambda: wait_all(rsend, 2, send_sem.at[0]))
        wait_all(cv, 2, send_sem.at[1])
        wait_all(ksend, 16, send_sem.at[3])


def spread(all_ref, rz_in, x_ref, r_ref, d_ref, rz_ref, sem):
    parts = [(all_ref.at[i], ref) for i, ref in enumerate((x_ref, r_ref, d_ref))]
    parts.append((rz_in, rz_ref))
    copies = [pltpu.make_async_copy(src, dst, sem.at[i]) for i, (src, dst) in enumerate(parts)]
    for one in copies:
        one.start()
    for one in copies:
        one.wait()


def solution(mesh):
    layers, cols = mesh.shape["layer"], mesh.shape["col"]

    def per_device(
        iterate,
        residual_in,
        direction_in,
        previous_rz,
        local_schur,
        local_inverse,
        coarse_inverse,
        face_included,
    ):
        _, _, _, fb, rhs = iterate.shape
        nb = 4 * fb
        nco = coarse_inverse.shape[1]
        n_late = min(layers, layers // 2 + 3) - max(1, layers // 2 - 1)
        f32 = jnp.float32
        x, q = iterate.reshape(nb, rhs), direction_in.reshape(nb, rhs)
        hbm = pl.BlockSpec(memory_space=pltpu.HBM)
        vmem = pl.BlockSpec(memory_space=pltpu.VMEM)
        field = jax.ShapeDtypeStruct((4, fb, rhs), f32)
        scalar = jax.ShapeDtypeStruct((1, rhs), f32)
        vec = pltpu.VMEM((nb, rhs), f32)
        mat = pltpu.VMEM((nb, nb), f32)
        wide = pltpu.VMEM((nb, 256), f32)
        every, rz = pl.pallas_call(
            functools.partial(kernel, layers, cols),
            out_shape=(pltpu.VMEM((3, 4, fb, rhs), f32), pltpu.VMEM((1, rhs), f32)),
            in_specs=[pl.BlockSpec(memory_space=pltpu.SMEM), vmem] + [hbm] * 6,
            out_specs=(vmem, vmem),
            scratch_shapes=[
                vec,
                vec,
                vec,
                mat,
                mat,
                pltpu.VMEM((2, nco), f32),
                wide,
                wide,
                vec,
                vec,
                pltpu.VMEM((3, 4, fb, rhs), f32),
                pltpu.VMEM((3, 4, fb, rhs), f32),
                pltpu.VMEM((2, rhs), f32),
                pltpu.VMEM((layers, 2, rhs), f32),
                pltpu.VMEM((layers, 2, nco), f32),
                pltpu.VMEM((128, nco), f32),
                pltpu.VMEM((nco, 128), f32),
                pltpu.VMEM((nco, 128), f32),
                pltpu.VMEM((cols, 2 * (layers - n_late), rhs), f32),
                pltpu.VMEM((cols, 2 * n_late, rhs), f32),
                pltpu.VMEM((16, rhs), f32),
                pltpu.VMEM((layers, 16, rhs), f32),
                pltpu.VMEM((layers, 4, rhs), f32),
                pltpu.VMEM((4, rhs), f32),
                pltpu.VMEM((128, rhs), f32),
                pltpu.VMEM((4, rhs), f32),
                pltpu.VMEM((cols, 4, rhs), f32),
                pltpu.VMEM((4, rhs), f32),
                pltpu.VMEM((4, rhs), f32),
                pltpu.SemaphoreType.DMA((9,)),
                pltpu.SemaphoreType.DMA((10,)),
                pltpu.SemaphoreType.DMA((10,)),
                pltpu.SemaphoreType.DMA((3,)),
                pltpu.SemaphoreType.DMA((3,)),
            ],
            compiler_params=pltpu.CompilerParams(
                collective_id=0, has_side_effects=True, vmem_limit_bytes=VMEM_LIMIT
            ),
        )(
            face_included.reshape(4),
            previous_rz.reshape(1, rhs),
            x,
            residual_in.reshape(4, fb, rhs),
            q,
            local_schur.reshape(nb, nb),
            local_inverse.reshape(nb, nb),
            coarse_inverse,
        )
        xo, ro, do, rz = pl.pallas_call(
            spread,
            out_shape=(field, field, field, scalar),
            in_specs=[vmem] * 2,
            out_specs=(hbm, hbm, hbm, hbm),
            scratch_shapes=[pltpu.SemaphoreType.DMA((4,))],
            compiler_params=pltpu.CompilerParams(vmem_limit_bytes=1024 * 1024),
        )(pltpu.with_memory_space_constraint(every, pltpu.VMEM), pltpu.with_memory_space_constraint(rz, pltpu.VMEM))
        shape = iterate.shape
        return xo.reshape(shape), ro.reshape(shape), do.reshape(shape), rz.reshape(rhs)

    placed = (
        P("layer", "col", None, None, None),
        P("layer", "col", None, None, None),
        P("layer", "col", None, None, None),
        P(),
        P("layer", "col", None, None),
        P("layer", "col", None, None),
        P(("layer", "col"), None),
        P("layer", "col", None),
    )
    return jax.shard_map(
        per_device,
        mesh=mesh,
        in_specs=placed,
        out_specs=(
            P("layer", "col", None, None, None),
            P("layer", "col", None, None, None),
            P("layer", "col", None, None, None),
            P(),
        ),
        check_vma=False,
    )
```

```python
import functools
import jax
import jax.numpy as jnp
from jax import lax
from jax.experimental import pallas as pl
from jax.experimental.pallas import tpu as pltpu
from jax.sharding import PartitionSpec as P

MESH = pl.DeviceIdType.MESH
HIGH = lax.Precision.HIGHEST
VMEM_LIMIT = 60 * 1024 * 1024


def mm(a, b):
    return jnp.dot(a, b, precision=HIGH, preferred_element_type=jnp.float32)


def wait_all(ref, count, sem):
    part = ref.at[pl.ds(0, count)]
    pltpu.make_async_copy(part, part, sem).wait()


def kernel(
    layers,
    cols,
    inc_ref,
    prz_ref,
    x_hbm,
    r_hbm,
    q_hbm,
    s_hbm,
    m_hbm,
    c_hbm,
    out_ref,
    rz_ref,
    xv,
    rv,
    qv,
    sv,
    mv,
    cv,
    rhs,
    sqe,
    spv,
    pd,
    hsrc,
    hdst,
    rsend,
    rbuf,
    rfar,
    cbuf,
    zmat,
    ct,
    turned,
    rall,
    rlate,
    ksend,
    kbuf,
    csend,
    crecv,
    cpad,
    a2send,
    a2buf,
    ssend,
    srecv,
    in_sem,
    send_sem,
    recv_sem,
    hsend_sem,
    hrecv_sem,
):
    fb = xv.shape[0] // 4
    width = 2 * cols
    nco = cv.shape[1]
    lanes = min(128, nco)
    lay = lax.axis_index("layer")
    col = lax.axis_index("col")
    below = lax.rem(lay + layers - 1, layers)
    above = lax.rem(lay + 1, layers)
    left = lax.rem(col + cols - 1, cols)
    right = lax.rem(col + 1, cols)
    center = lay == 0
    pair, core = col // 2, lax.rem(col, 2)
    twin = 2 * pair + 1 - core
    outer = lay != 0
    top = lay == layers - 1
    inside = outer & (lay != layers - 1)
    first, last = max(1, layers // 2 - 1), min(layers, layers // 2 + 3)
    late = list(range(first, last))
    early = [l for l in range(layers) if l not in late]
    near = min(4, layers)
    far = (lay >= first) & (lay < last)

    def face(f):
        return pl.ds(f * fb, fb)

    def load(src, dst, i):
        return pltpu.make_async_copy(src, dst, in_sem.at[i])

    loads = [
        load(r_hbm.at[1], rv.at[face(1), :], 0),
        load(c_hbm, cv, 1),
        load(m_hbm, mv, 2),
        load(q_hbm, qv, 3),
        load(s_hbm, sv, 4),
        load(x_hbm, xv, 5),
        load(r_hbm.at[3], rv.at[face(3), :], 6),
        load(r_hbm.at[0], rv.at[face(0), :], 7),
        load(r_hbm.at[2], rv.at[face(2), :], 8),
    ]
    loads[0].start()
    loads[6].start()

    barrier = pltpu.get_barrier_semaphore()

    def greet(l, c):
        pl.semaphore_signal(barrier, inc=1, device_id=(l, c), device_id_type=MESH)

    def others(n, me, act):
        def body(k, carry):
            act(lax.rem(me + k, n))
            return carry

        lax.fori_loop(1, n, body, 0)

    def first_ones(n, me, heads, act):
        for h in range(heads):
            pl.when(me != h)(functools.partial(act, h))

        def rest(p):
            pl.when(p >= heads)(lambda: act(p))

        others(n, me, rest)

    def send(src, dst, i, l, c):
        pltpu.make_async_remote_copy(
            src_ref=src,
            dst_ref=dst,
            send_sem=send_sem.at[i],
            recv_sem=recv_sem.at[i],
            device_id=(l, c),
            device_id_type=MESH,
        ).start()

    greet(lay, left)
    greet(lay, right)
    pl.when(outer)(lambda: greet(below, col))
    pl.when(jnp.logical_not(top))(lambda: greet(above, col))
    for i in (7, 8, 1, 2, 3, 4, 5):
        loads[i].start()

    @pl.when(center)
    def _():
        others(layers, lay, lambda l: greet(l, col))
        others(layers, lay, lambda l: greet(l, twin))
        others(cols, col, lambda c: greet(lay, c))

    def halo(i):
        def one(f, g, l, c):
            pltpu.make_async_remote_copy(
                src_ref=hsrc.at[i, f],
                dst_ref=hdst.at[i, g],
                send_sem=hsend_sem.at[i],
                recv_sem=hrecv_sem.at[i],
                device_id=(l, c),
                device_id_type=MESH,
            ).start()

        pl.when(outer)(lambda: one(0, 1, below, col))
        pl.when(jnp.logical_not(top))(lambda: one(1, 0, above, col))
        one(2, 3, lay, left)
        one(3, 2, lay, right)

    def halo_wait(i, sem):
        pl.when(inside)(lambda: wait_all(hdst.at[i], 4, sem.at[i]))
        pl.when(jnp.logical_not(inside))(lambda: wait_all(hdst.at[i], 3, sem.at[i]))

    def assembled(i, own, f):
        got = hdst[i, f]
        if f == 0:
            got = jnp.where(lay > 0, got, 0.0)
        if f == 1:
            got = jnp.where(lay < layers - 1, got, 0.0)
        return own + got

    inc = [inc_ref[f].astype(jnp.float32) for f in range(4)]
    cpad[...] = jnp.zeros_like(cpad)

    means = {}

    def average(f, i):
        loads[i].wait()
        res = inc[f] * rv[face(f), :]
        rv[face(f), :] = res
        means[f] = jnp.mean(res, axis=0, keepdims=True)
        spv[face(f), :] = 0.5 * (res - means[f])

    average(1, 0)
    average(3, 6)
    rsend[0:1, :] = means[1]
    rsend[1:2, :] = means[3]

    @pl.when(center)
    def _():
        zmat[3 * layers :, :] = jnp.zeros((zmat.shape[0] - 3 * layers, nco), jnp.float32)
        rbuf[0] = rsend[...]
        loads[1].wait()
        cbuf[0] = cv[...]
    @pl.when(outer)
    def _():
        pl.when(top)(lambda: pl.semaphore_wait(barrier, 5))
        pl.when(inside)(lambda: pl.semaphore_wait(barrier, 6))

        @pl.when(far)
        def _():
            send(rsend, rfar.at[core, lay - first], 8, 0, col)
            send(rsend, rfar.at[core, lay - first], 8, 0, twin)

        @pl.when(jnp.logical_not(far))
        def _():
            send(rsend, rbuf.at[lay], 0, 0, col)

        loads[1].wait()
        send(cv, cbuf.at[lay], 1, 0, col)

    average(0, 7)
    average(2, 8)
    loads[2].wait()
    inner = mm(mv[...], spv[...])
    rz = jnp.zeros_like(means[0])
    for f in range(4):
        part = inner[f * fb : (f + 1) * fb]
        half = 0.5 * (inc[f] * (part - jnp.mean(part, axis=0, keepdims=True)))
        hsrc[0, f] = half
        rz += jnp.sum(rv[face(f), :] * half, axis=0, keepdims=True)
    pl.when(outer)(lambda: halo(0))
    ksend[8:9, :] = rz

    loads[3].wait()
    lane = lax.broadcasted_iota(jnp.int32, (fb, 128), 1)
    for f in range(4):
        prev = inc[f] * qv[face(f), :]
        qv[face(f), :] = prev
        rhs[face(f), 0:128] = prev
        rhs[face(f), 128:256] = jnp.where(lane == f, inc[f], 0.0)
    loads[4].wait()
    sqe[...] = mm(sv[...], rhs[...])
    qq = jnp.zeros_like(rz)
    for f in range(4):
        sq = inc[f] * sqe[face(f), 0:128]
        se = inc[f] * sqe[face(f), 128:256]
        sqe[face(f), 128:256] = se
        hsrc[1, f] = sq
        qq += jnp.sum(qv[face(f), :] * sq, axis=0, keepdims=True)
        ksend[4 + f : 5 + f, :] = 2.0 * jnp.sum(sq, axis=0, keepdims=True)
        ksend[12 + f : 13 + f, :] = jnp.sum(se, axis=0, keepdims=True)
    pl.when(outer)(lambda: halo(1))
    ksend[11:12, :] = qq

    @pl.when(center)
    def _():
        pl.semaphore_wait(barrier, 3 + cols - 1)
        halo(0)
        halo(1)

    halo_wait(0, hrecv_sem)
    for f in range(4):
        pd[face(f), :] = assembled(0, hsrc[0, f], f)
    spv[...] = mm(sv[...], pd[...])
    pp = jnp.zeros_like(rz)
    pq = jnp.zeros_like(rz)
    for f in range(4):
        sp = inc[f] * spv[face(f), :]
        spv[face(f), :] = sp
        here = pd[face(f), :]
        pp += jnp.sum(here * sp, axis=0, keepdims=True)
        pq += jnp.sum(here * hsrc[1, f], axis=0, keepdims=True)
        ksend[f : f + 1, :] = 2.0 * jnp.sum(sp, axis=0, keepdims=True)
    ksend[9:10, :] = pp
    ksend[10:11, :] = 2.0 * pq

    @pl.when(outer)
    def _():
        send(ksend, kbuf.at[lay], 3, 0, col)

    @pl.when(center)
    def _():
        wait_all(rbuf, len(early) - 1, recv_sem.at[0])
        for i, l in enumerate(early):
            for g in range(2):
                at = g * len(early) + i
                rall[pair, core, at : at + 1, :] = rbuf[l, g : g + 1, :]
        mine = rall.at[pair, core]
        others(cols // 2, pair, lambda p: send(mine, mine, 2, 0, 2 * p + core))
        wait_all(rfar, 2, recv_sem.at[8])
        for i, l in enumerate(late):
            for k in range(2):
                for g in range(2):
                    at = g * len(late) + i
                    rlate[pair, k, at : at + 1, :] = rfar[k, i, g : g + 1, :]
        both = rlate.at[pair]
        first_ones(cols // 2, pair, 1, lambda p: send(both, both, 9, 0, 2 * p + core))
        for i, l in enumerate(late):
            rbuf[l] = rfar[core, i]
        wait_all(cbuf, layers - 1, recv_sem.at[1])
        for l in range(layers):
            for g in range(2):
                zmat[g * layers + l : g * layers + l + 1, :] = cbuf[l, g : g + 1, :]
        mid = zmat.at[pl.ds(layers, layers)]
        send(mid, zmat.at[pl.ds(2 * layers, layers)], 7, 0, right)
        wait_all(rall.at[:, 0], cols // 2 - 1, recv_sem.at[2])
        half = rall.at[:, core]
        send(half, half, 10, 0, twin)

    @pl.when(center)
    def _():
        wait_all(zmat, layers, recv_sem.at[7])
        wait_all(zmat, layers, send_sem.at[7])
        for j in range(nco // lanes):
            ct[j * lanes : (j + 1) * lanes, :] = zmat[:, j * lanes : (j + 1) * lanes].T
        for c in range(cols):
            for g in range(2):
                at = (2 * c + g) * len(early)
                end = 2 * cols * len(early) + (2 * c + g) * len(late)
                for src, dst, n in (
                    (0, at, first),
                    (last, at + first, layers - last),
                    (first, end, len(late)),
                ):
                    if n:
                        rows = ct[pl.ds(src * width + 2 * c + g, n, stride=width), :]
                        turned[dst : dst + n, :] = rows
        for j in range(nco // lanes):
            zmat[:, j * lanes : (j + 1) * lanes] = turned[j * lanes : (j + 1) * lanes, :].T

    halo_wait(1, hrecv_sem)
    for f in range(4):
        sqe[face(f), 0:128] = assembled(1, hsrc[1, f], f)
    loads[5].wait()

    @pl.when(center)
    def _():
        kbuf[0] = ksend[...]
        wait_all(rall.at[:, 0], cols // 2, recv_sem.at[10])
        cut = 2 * cols * len(early)
        total = mm(zmat[0 : 3 * layers, 0:cut], rall[...].reshape(cut, rall.shape[3]))
        wait_all(rlate, cols // 2 - 1, recv_sem.at[9])
        rest = rlate[...].reshape(nco - cut, rlate.shape[3])
        total += mm(zmat[0 : 3 * layers, cut:nco], rest)
        for l in range(layers):
            low = (l + layers - 1) % layers
            csend[l, 0:1, :] = total[low : low + 1]
            csend[l, 1:2, :] = total[l : l + 1]
            csend[l, 2:3, :] = total[2 * layers + l : 2 * layers + l + 1]
            csend[l, 3:4, :] = total[layers + l : layers + l + 1]
        for l in range(1, near):
            send(csend.at[l], crecv, 4, l, col)
        wait_all(kbuf, layers - 1, recv_sem.at[3])
        base = jnp.zeros_like(a2send)
        quad = jnp.zeros_like(a2send)
        cross = jnp.zeros_like(a2send)
        work = jnp.zeros((1, a2send.shape[1]), jnp.float32)
        for l in range(layers):
            cor = csend[l]
            mixed = kbuf[l, 0:4, :]
            block = kbuf[l, 12:16, :]
            for g in range(4):
                mixed += block[:, g : g + 1] * cor[g : g + 1]
            quad += cor * mixed
            cross += cor * kbuf[l, 4:8, :]
            base += kbuf[l, 8:12, :]
            work += rbuf[l, 0:1, :] * cor[1:2] + rbuf[l, 1:2, :] * cor[3:4]
        a2send[0:1, :] = base[0:1] + float(fb) * work
        a2send[1:2, :] = base[1:2] + jnp.sum(quad, axis=0, keepdims=True)
        a2send[2:3, :] = base[2:3] + jnp.sum(cross, axis=0, keepdims=True)
        a2send[3:4, :] = base[3:4]
        first_ones(cols, col, 2, lambda c: send(a2send, a2buf.at[col], 5, 0, c))
        a2buf[pl.ds(col, 1)] = a2send[...][None]
        crecv[...] = csend[0]
        for l in range(near, layers):
            send(csend.at[l], crecv, 4, l, col)

    @pl.when(outer)
    def _():
        wait_all(crecv, 4, recv_sem.at[4])

    cor = [inc[f] * crecv[f : f + 1, :] for f in range(4)]
    for f in range(4):
        cpad[f : f + 1, :] = cor[f]
    change = mm(sqe[:, 128:256], cpad[...])
    for f in range(4):
        hsrc[2, f] = spv[face(f), :] + change[f * fb : (f + 1) * fb]
    halo(2)
    for f in range(4):
        pd[face(f), :] = pd[face(f), :] + cor[f]

    @pl.when(center)
    def _():
        wait_all(a2buf, cols - 1, recv_sem.at[5])
        ssend[...] = jnp.sum(a2buf[...], axis=0)
        for l in range(1, layers):
            send(ssend, srecv, 6, l, col)
        srecv[...] = ssend[...]

    halo_wait(2, hrecv_sem)
    for f in range(4):
        spv[face(f), :] = assembled(2, hsrc[2, f], f)

    @pl.when(outer)
    def _():
        wait_all(srecv, 4, recv_sem.at[6])

    sums = srecv[...]
    rz_all = sums[0:1]
    beta = rz_all / prz_ref[...]
    curvature = sums[1:2] + beta * (sums[2:3] + beta * sums[3:4])
    alpha = rz_all / curvature
    rz_ref[...] = rz_all
    for f in range(4):
        direction = pd[face(f), :] + beta * qv[face(f), :]
        out_ref[2, f] = direction
        out_ref[0, f] = xv[face(f), :] + alpha * direction
        image = spv[face(f), :] + beta * sqe[face(f), 0:128]
        out_ref[1, f] = rv[face(f), :] - alpha * image

    for i in range(3):
        halo_wait(i, hsend_sem)

    @pl.when(center)
    def _():
        wait_all(rall.at[:, 0], cols // 2 - 1, send_sem.at[2])
        wait_all(rall.at[:, 0], cols // 2, send_sem.at[10])
        wait_all(rlate, cols // 2 - 1, send_sem.at[9])
        wait_all(csend, layers - 1, send_sem.at[4])
        wait_all(a2buf, cols - 1, send_sem.at[5])
        wait_all(csend, layers - 1, send_sem.at[6])

    @pl.when(outer)
    def _():
        pl.when(far)(lambda: wait_all(rfar.at[0], 2, send_sem.at[8]))
        pl.when(jnp.logical_not(far))(lambda: wait_all(rsend, 2, send_sem.at[0]))
        wait_all(cv, 2, send_sem.at[1])
        wait_all(ksend, 16, send_sem.at[3])


def spread(all_ref, rz_in, x_ref, r_ref, d_ref, rz_ref, sem):
    parts = [(all_ref.at[i], ref) for i, ref in enumerate((x_ref, r_ref, d_ref))]
    parts.append((rz_in, rz_ref))
    copies = [pltpu.make_async_copy(src, dst, sem.at[i]) for i, (src, dst) in enumerate(parts)]
    for one in copies:
        one.start()
    for one in copies:
        one.wait()


def solution(mesh):
    layers, cols = mesh.shape["layer"], mesh.shape["col"]

    def per_device(
        iterate,
        residual_in,
        direction_in,
        previous_rz,
        local_schur,
        local_inverse,
        coarse_inverse,
        face_included,
    ):
        _, _, _, fb, rhs = iterate.shape
        nb = 4 * fb
        nco = coarse_inverse.shape[1]
        n_late = min(layers, layers // 2 + 3) - max(1, layers // 2 - 1)
        f32 = jnp.float32
        x, q = iterate.reshape(nb, rhs), direction_in.reshape(nb, rhs)
        hbm = pl.BlockSpec(memory_space=pltpu.HBM)
        vmem = pl.BlockSpec(memory_space=pltpu.VMEM)
        field = jax.ShapeDtypeStruct((4, fb, rhs), f32)
        scalar = jax.ShapeDtypeStruct((1, rhs), f32)
        vec = pltpu.VMEM((nb, rhs), f32)
        mat = pltpu.VMEM((nb, nb), f32)
        wide = pltpu.VMEM((nb, 256), f32)
        every, rz = pl.pallas_call(
            functools.partial(kernel, layers, cols),
            out_shape=(pltpu.VMEM((3, 4, fb, rhs), f32), pltpu.VMEM((1, rhs), f32)),
            in_specs=[pl.BlockSpec(memory_space=pltpu.SMEM), vmem] + [hbm] * 6,
            out_specs=(vmem, vmem),
            scratch_shapes=[
                vec,
                vec,
                vec,
                mat,
                mat,
                pltpu.VMEM((2, nco), f32),
                wide,
                wide,
                vec,
                vec,
                pltpu.VMEM((3, 4, fb, rhs), f32),
                pltpu.VMEM((3, 4, fb, rhs), f32),
                pltpu.VMEM((2, rhs), f32),
                pltpu.VMEM((layers, 2, rhs), f32),
                pltpu.VMEM((2, n_late, 2, rhs), f32),
                pltpu.VMEM((layers, 2, nco), f32),
                pltpu.VMEM((128, nco), f32),
                pltpu.VMEM((nco, 128), f32),
                pltpu.VMEM((nco, 128), f32),
                pltpu.VMEM((cols // 2, 2, 2 * (layers - n_late), rhs), f32),
                pltpu.VMEM((cols // 2, 2, 2 * n_late, rhs), f32),
                pltpu.VMEM((16, rhs), f32),
                pltpu.VMEM((layers, 16, rhs), f32),
                pltpu.VMEM((layers, 4, rhs), f32),
                pltpu.VMEM((4, rhs), f32),
                pltpu.VMEM((128, rhs), f32),
                pltpu.VMEM((4, rhs), f32),
                pltpu.VMEM((cols, 4, rhs), f32),
                pltpu.VMEM((4, rhs), f32),
                pltpu.VMEM((4, rhs), f32),
                pltpu.SemaphoreType.DMA((9,)),
                pltpu.SemaphoreType.DMA((11,)),
                pltpu.SemaphoreType.DMA((11,)),
                pltpu.SemaphoreType.DMA((3,)),
                pltpu.SemaphoreType.DMA((3,)),
            ],
            compiler_params=pltpu.CompilerParams(
                collective_id=0, has_side_effects=True, vmem_limit_bytes=VMEM_LIMIT
            ),
        )(
            face_included.reshape(4),
            previous_rz.reshape(1, rhs),
            x,
            residual_in.reshape(4, fb, rhs),
            q,
            local_schur.reshape(nb, nb),
            local_inverse.reshape(nb, nb),
            coarse_inverse,
        )
        xo, ro, do, rz = pl.pallas_call(
            spread,
            out_shape=(field, field, field, scalar),
            in_specs=[vmem] * 2,
            out_specs=(hbm, hbm, hbm, hbm),
            scratch_shapes=[pltpu.SemaphoreType.DMA((4,))],
            compiler_params=pltpu.CompilerParams(vmem_limit_bytes=1024 * 1024),
        )(pltpu.with_memory_space_constraint(every, pltpu.VMEM), pltpu.with_memory_space_constraint(rz, pltpu.VMEM))
        shape = iterate.shape
        return xo.reshape(shape), ro.reshape(shape), do.reshape(shape), rz.reshape(rhs)

    placed = (
        P("layer", "col", None, None, None),
        P("layer", "col", None, None, None),
        P("layer", "col", None, None, None),
        P(),
        P("layer", "col", None, None),
        P("layer", "col", None, None),
        P(("layer", "col"), None),
        P("layer", "col", None),
    )
    return jax.shard_map(
        per_device,
        mesh=mesh,
        in_specs=placed,
        out_specs=(
            P("layer", "col", None, None, None),
            P("layer", "col", None, None, None),
            P("layer", "col", None, None, None),
            P(),
        ),
        check_vma=False,
    )
```

```python
import functools
import jax
import jax.numpy as jnp
from jax import lax
from jax.experimental import pallas as pl
from jax.experimental.pallas import tpu as pltpu
from jax.sharding import PartitionSpec as P

MESH = pl.DeviceIdType.MESH
HIGH = lax.Precision.HIGHEST
VMEM_LIMIT = 60 * 1024 * 1024


def mm(a, b):
    return jnp.dot(a, b, precision=HIGH, preferred_element_type=jnp.float32)


def wait_all(ref, count, sem):
    part = ref.at[pl.ds(0, count)]
    pltpu.make_async_copy(part, part, sem).wait()


def kernel(
    layers,
    cols,
    inc_ref,
    prz_ref,
    x_hbm,
    r_hbm,
    q_hbm,
    s_hbm,
    m_hbm,
    c_hbm,
    out_ref,
    rz_ref,
    xv,
    rv,
    qv,
    sv,
    mv,
    cv,
    rhs,
    sqe,
    spv,
    pd,
    hsrc,
    hdst,
    rsend,
    rbuf,
    rfar,
    cbuf,
    zmat,
    ct,
    turned,
    rall,
    rlate,
    ksend,
    kbuf,
    csend,
    crecv,
    cpad,
    a2send,
    a2buf,
    ssend,
    srecv,
    in_sem,
    send_sem,
    recv_sem,
    hsend_sem,
    hrecv_sem,
):
    fb = xv.shape[0] // 4
    width = 2 * cols
    nco = cv.shape[1]
    lanes = min(128, nco)
    lay = lax.axis_index("layer")
    col = lax.axis_index("col")
    below = lax.rem(lay + layers - 1, layers)
    above = lax.rem(lay + 1, layers)
    left = lax.rem(col + cols - 1, cols)
    right = lax.rem(col + 1, cols)
    center = lay == 0
    pair, core = col // 2, lax.rem(col, 2)
    twin = 2 * pair + 1 - core
    outer = lay != 0
    top = lay == layers - 1
    inside = outer & (lay != layers - 1)
    first, last = max(1, layers // 2 - 1), min(layers, layers // 2 + 3)
    late = list(range(first, last))
    early = [l for l in range(layers) if l not in late]
    near = min(4, layers)
    far = (lay >= first) & (lay < last)

    def face(f):
        return pl.ds(f * fb, fb)

    def load(src, dst, i):
        return pltpu.make_async_copy(src, dst, in_sem.at[i])

    loads = [
        load(r_hbm.at[1], rv.at[face(1), :], 0),
        load(c_hbm, cv, 1),
        load(m_hbm, mv, 2),
        load(q_hbm, qv, 3),
        load(s_hbm, sv, 4),
        load(x_hbm, xv, 5),
        load(r_hbm.at[3], rv.at[face(3), :], 6),
        load(r_hbm.at[0], rv.at[face(0), :], 7),
        load(r_hbm.at[2], rv.at[face(2), :], 8),
    ]
    loads[0].start()
    loads[6].start()

    barrier = pltpu.get_barrier_semaphore()

    def greet(l, c):
        pl.semaphore_signal(barrier, inc=1, device_id=(l, c), device_id_type=MESH)

    def others(n, me, act):
        def body(k, carry):
            act(lax.rem(me + k, n))
            return carry

        lax.fori_loop(1, n, body, 0)

    def first_ones(n, me, heads, act):
        for h in range(heads):
            pl.when(me != h)(functools.partial(act, h))

        def rest(p):
            pl.when(p >= heads)(lambda: act(p))

        others(n, me, rest)

    def send(src, dst, i, l, c):
        pltpu.make_async_remote_copy(
            src_ref=src,
            dst_ref=dst,
            send_sem=send_sem.at[i],
            recv_sem=recv_sem.at[i],
            device_id=(l, c),
            device_id_type=MESH,
        ).start()

    greet(lay, left)
    greet(lay, right)
    pl.when(outer)(lambda: greet(below, col))
    pl.when(jnp.logical_not(top))(lambda: greet(above, col))
    for i in (7, 8, 1, 2, 3, 4, 5):
        loads[i].start()

    @pl.when(center)
    def _():
        others(layers, lay, lambda l: greet(l, col))
        others(layers, lay, lambda l: greet(l, twin))
        others(cols, col, lambda c: greet(lay, c))

    def halo(i):
        def one(f, g, l, c):
            pltpu.make_async_remote_copy(
                src_ref=hsrc.at[i, f],
                dst_ref=hdst.at[i, g],
                send_sem=hsend_sem.at[i],
                recv_sem=hrecv_sem.at[i],
                device_id=(l, c),
                device_id_type=MESH,
            ).start()

        pl.when(outer)(lambda: one(0, 1, below, col))
        pl.when(jnp.logical_not(top))(lambda: one(1, 0, above, col))
        one(2, 3, lay, left)
        one(3, 2, lay, right)

    def halo_wait(i, sem):
        pl.when(inside)(lambda: wait_all(hdst.at[i], 4, sem.at[i]))
        pl.when(jnp.logical_not(inside))(lambda: wait_all(hdst.at[i], 3, sem.at[i]))

    def assembled(i, own, f):
        got = hdst[i, f]
        if f == 0:
            got = jnp.where(lay > 0, got, 0.0)
        if f == 1:
            got = jnp.where(lay < layers - 1, got, 0.0)
        return own + got

    inc = [inc_ref[f].astype(jnp.float32) for f in range(4)]
    cpad[...] = jnp.zeros_like(cpad)

    means = {}

    def average(f, i):
        loads[i].wait()
        res = inc[f] * rv[face(f), :]
        rv[face(f), :] = res
        means[f] = jnp.mean(res, axis=0, keepdims=True)
        spv[face(f), :] = 0.5 * (res - means[f])

    average(1, 0)
    average(3, 6)
    rsend[0:1, :] = means[1]
    rsend[1:2, :] = means[3]

    @pl.when(center)
    def _():
        zmat[3 * layers :, :] = jnp.zeros((zmat.shape[0] - 3 * layers, nco), jnp.float32)
        rbuf[0] = rsend[...]
        loads[1].wait()
        cbuf[0] = cv[...]
    @pl.when(outer)
    def _():
        pl.when(top)(lambda: pl.semaphore_wait(barrier, 5))
        pl.when(inside)(lambda: pl.semaphore_wait(barrier, 6))

        @pl.when(far)
        def _():
            send(rsend, rfar.at[core, lay - first], 8, 0, col)
            send(rsend, rfar.at[core, lay - first], 8, 0, twin)

        @pl.when(jnp.logical_not(far))
        def _():
            send(rsend, rbuf.at[lay], 0, 0, col)

        loads[1].wait()
        send(cv, cbuf.at[lay], 1, 0, col)

    average(0, 7)
    average(2, 8)
    loads[2].wait()
    inner = mm(mv[...], spv[...])
    rz = jnp.zeros_like(means[0])
    for f in range(4):
        part = inner[f * fb : (f + 1) * fb]
        half = 0.5 * (inc[f] * (part - jnp.mean(part, axis=0, keepdims=True)))
        hsrc[0, f] = half
        rz += jnp.sum(rv[face(f), :] * half, axis=0, keepdims=True)
    pl.when(outer)(lambda: halo(0))
    ksend[8:9, :] = rz

    loads[3].wait()
    lane = lax.broadcasted_iota(jnp.int32, (fb, 128), 1)
    for f in range(4):
        prev = inc[f] * qv[face(f), :]
        qv[face(f), :] = prev
        rhs[face(f), 0:128] = prev
        rhs[face(f), 128:256] = jnp.where(lane == f, inc[f], 0.0)
    loads[4].wait()
    sqe[...] = mm(sv[...], rhs[...])
    qq = jnp.zeros_like(rz)
    for f in range(4):
        sq = inc[f] * sqe[face(f), 0:128]
        se = inc[f] * sqe[face(f), 128:256]
        sqe[face(f), 128:256] = se
        hsrc[1, f] = sq
        qq += jnp.sum(qv[face(f), :] * sq, axis=0, keepdims=True)
        ksend[4 + f : 5 + f, :] = 2.0 * jnp.sum(sq, axis=0, keepdims=True)
        ksend[12 + f : 13 + f, :] = jnp.sum(se, axis=0, keepdims=True)
    pl.when(outer)(lambda: halo(1))
    ksend[11:12, :] = qq

    @pl.when(center)
    def _():
        pl.semaphore_wait(barrier, 3 + cols - 1)
        halo(0)
        halo(1)

    halo_wait(0, hrecv_sem)
    for f in range(4):
        pd[face(f), :] = assembled(0, hsrc[0, f], f)
    spv[...] = mm(sv[...], pd[...])
    pp = jnp.zeros_like(rz)
    pq = jnp.zeros_like(rz)
    for f in range(4):
        sp = inc[f] * spv[face(f), :]
        spv[face(f), :] = sp
        here = pd[face(f), :]
        pp += jnp.sum(here * sp, axis=0, keepdims=True)
        pq += jnp.sum(here * hsrc[1, f], axis=0, keepdims=True)
        ksend[f : f + 1, :] = 2.0 * jnp.sum(sp, axis=0, keepdims=True)
    ksend[9:10, :] = pp
    ksend[10:11, :] = 2.0 * pq

    @pl.when(outer)
    def _():
        send(ksend, kbuf.at[lay], 3, 0, col)

    @pl.when(center)
    def _():
        wait_all(rbuf, len(early) - 1, recv_sem.at[0])
        for i, l in enumerate(early):
            for g in range(2):
                at = g * len(early) + i
                rall[pair, core, at : at + 1, :] = rbuf[l, g : g + 1, :]
        mine = rall.at[pair, core]
        others(cols // 2, pair, lambda p: send(mine, mine, 2, 0, 2 * p + core))
        wait_all(rfar, 2, recv_sem.at[8])
        for i, l in enumerate(late):
            for k in range(2):
                for g in range(2):
                    at = g * len(late) + i
                    rlate[pair, k, at : at + 1, :] = rfar[k, i, g : g + 1, :]
        both = rlate.at[pair]
        first_ones(cols // 2, pair, 1, lambda p: send(both, both, 9, 0, 2 * p + core))
        for i, l in enumerate(late):
            rbuf[l] = rfar[core, i]
        wait_all(cbuf, layers - 1, recv_sem.at[1])
        for l in range(layers):
            for g in range(2):
                zmat[g * layers + l : g * layers + l + 1, :] = cbuf[l, g : g + 1, :]
        mid = zmat.at[pl.ds(layers, layers)]
        send(mid, zmat.at[pl.ds(2 * layers, layers)], 7, 0, right)
        wait_all(rall.at[:, 0], cols // 2 - 1, recv_sem.at[2])
        half = rall.at[:, core]
        send(half, half, 10, 0, twin)

    @pl.when(center)
    def _():
        wait_all(zmat, layers, recv_sem.at[7])
        wait_all(zmat, layers, send_sem.at[7])
        for j in range(nco // lanes):
            ct[j * lanes : (j + 1) * lanes, :] = zmat[:, j * lanes : (j + 1) * lanes].T
        for c in range(cols):
            for g in range(2):
                at = (2 * c + g) * len(early)
                end = 2 * cols * len(early) + (2 * c + g) * len(late)
                for src, dst, n in (
                    (0, at, first),
                    (last, at + first, layers - last),
                    (first, end, len(late)),
                ):
                    if n:
                        rows = ct[pl.ds(src * width + 2 * c + g, n, stride=width), :]
                        turned[dst : dst + n, :] = rows
        for j in range(nco // lanes):
            zmat[:, j * lanes : (j + 1) * lanes] = turned[j * lanes : (j + 1) * lanes, :].T

    halo_wait(1, hrecv_sem)
    for f in range(4):
        sqe[face(f), 0:128] = assembled(1, hsrc[1, f], f)
    loads[5].wait()

    @pl.when(center)
    def _():
        kbuf[0] = ksend[...]
        wait_all(rall.at[:, 0], cols // 2, recv_sem.at[10])
        cut = 2 * cols * len(early)
        total = mm(zmat[0 : 3 * layers, 0:cut], rall[...].reshape(cut, rall.shape[3]))
        wait_all(rlate, cols // 2 - 1, recv_sem.at[9])
        rest = rlate[...].reshape(nco - cut, rlate.shape[3])
        total += mm(zmat[0 : 3 * layers, cut:nco], rest)
        for l in range(layers):
            low = (l + layers - 1) % layers
            csend[l, 0:1, :] = total[low : low + 1]
            csend[l, 1:2, :] = total[l : l + 1]
            csend[l, 2:3, :] = total[2 * layers + l : 2 * layers + l + 1]
            csend[l, 3:4, :] = total[layers + l : layers + l + 1]
        for l in range(1, near):
            send(csend.at[l], crecv, 4, l, col)
        wait_all(kbuf, layers - 1, recv_sem.at[3])
        base = jnp.zeros_like(a2send)
        quad = jnp.zeros_like(a2send)
        cross = jnp.zeros_like(a2send)
        work = jnp.zeros((1, a2send.shape[1]), jnp.float32)
        for l in range(layers):
            cor = csend[l]
            mixed = kbuf[l, 0:4, :]
            block = kbuf[l, 12:16, :]
            for g in range(4):
                mixed += block[:, g : g + 1] * cor[g : g + 1]
            quad += cor * mixed
            cross += cor * kbuf[l, 4:8, :]
            base += kbuf[l, 8:12, :]
            work += rbuf[l, 0:1, :] * cor[1:2] + rbuf[l, 1:2, :] * cor[3:4]
        a2send[0:1, :] = base[0:1] + float(fb) * work
        a2send[1:2, :] = base[1:2] + jnp.sum(quad, axis=0, keepdims=True)
        a2send[2:3, :] = base[2:3] + jnp.sum(cross, axis=0, keepdims=True)
        a2send[3:4, :] = base[3:4]
        first_ones(cols, col, 2, lambda c: send(a2send, a2buf.at[col], 5, 0, c))
        a2buf[pl.ds(col, 1)] = a2send[...][None]
        crecv[...] = csend[0]
        for l in range(near, layers):
            send(csend.at[l], crecv, 4, l, col)

    @pl.when(outer)
    def _():
        wait_all(crecv, 4, recv_sem.at[4])

    cor = [inc[f] * crecv[f : f + 1, :] for f in range(4)]
    for f in range(4):
        cpad[f : f + 1, :] = cor[f]
    change = mm(sqe[:, 128:256], cpad[...])
    for f in range(4):
        hsrc[2, f] = spv[face(f), :] + change[f * fb : (f + 1) * fb]
    halo(2)
    for f in range(4):
        pd[face(f), :] = pd[face(f), :] + cor[f]

    for i in range(3):
        halo_wait(i, hsend_sem)

    @pl.when(center)
    def _():
        wait_all(rall.at[:, 0], cols // 2 - 1, send_sem.at[2])
        wait_all(rall.at[:, 0], cols // 2, send_sem.at[10])
        wait_all(rlate, cols // 2 - 1, send_sem.at[9])
        wait_all(csend, layers - 1, send_sem.at[4])
        wait_all(a2buf, cols - 1, send_sem.at[5])

    @pl.when(outer)
    def _():
        pl.when(far)(lambda: wait_all(rfar.at[0], 2, send_sem.at[8]))
        pl.when(jnp.logical_not(far))(lambda: wait_all(rsend, 2, send_sem.at[0]))
        wait_all(cv, 2, send_sem.at[1])
        wait_all(ksend, 16, send_sem.at[3])

    @pl.when(center)
    def _():
        wait_all(a2buf, cols - 1, recv_sem.at[5])
        ssend[...] = jnp.sum(a2buf[...], axis=0)
        for l in range(1, layers):
            send(ssend, srecv, 6, l, col)
        srecv[...] = ssend[...]

    halo_wait(2, hrecv_sem)
    for f in range(4):
        spv[face(f), :] = assembled(2, hsrc[2, f], f)

    @pl.when(outer)
    def _():
        wait_all(srecv, 4, recv_sem.at[6])

    sums = srecv[...]
    rz_all = sums[0:1]
    beta = rz_all / prz_ref[...]
    curvature = sums[1:2] + beta * (sums[2:3] + beta * sums[3:4])
    alpha = rz_all / curvature
    rz_ref[...] = rz_all
    for f in range(4):
        direction = pd[face(f), :] + beta * qv[face(f), :]
        out_ref[2, f] = direction
        out_ref[0, f] = xv[face(f), :] + alpha * direction
        image = spv[face(f), :] + beta * sqe[face(f), 0:128]
        out_ref[1, f] = rv[face(f), :] - alpha * image

    @pl.when(center)
    def _():
        wait_all(csend, layers - 1, send_sem.at[6])


def spread(all_ref, rz_in, x_ref, r_ref, d_ref, rz_ref, sem):
    parts = [(all_ref.at[i], ref) for i, ref in enumerate((x_ref, r_ref, d_ref))]
    parts.append((rz_in, rz_ref))
    copies = [pltpu.make_async_copy(src, dst, sem.at[i]) for i, (src, dst) in enumerate(parts)]
    for one in copies:
        one.start()
    for one in copies:
        one.wait()


def solution(mesh):
    layers, cols = mesh.shape["layer"], mesh.shape["col"]

    def per_device(
        iterate,
        residual_in,
        direction_in,
        previous_rz,
        local_schur,
        local_inverse,
        coarse_inverse,
        face_included,
    ):
        _, _, _, fb, rhs = iterate.shape
        nb = 4 * fb
        nco = coarse_inverse.shape[1]
        n_late = min(layers, layers // 2 + 3) - max(1, layers // 2 - 1)
        f32 = jnp.float32
        x, q = iterate.reshape(nb, rhs), direction_in.reshape(nb, rhs)
        hbm = pl.BlockSpec(memory_space=pltpu.HBM)
        vmem = pl.BlockSpec(memory_space=pltpu.VMEM)
        field = jax.ShapeDtypeStruct((4, fb, rhs), f32)
        scalar = jax.ShapeDtypeStruct((1, rhs), f32)
        vec = pltpu.VMEM((nb, rhs), f32)
        mat = pltpu.VMEM((nb, nb), f32)
        wide = pltpu.VMEM((nb, 256), f32)
        every, rz = pl.pallas_call(
            functools.partial(kernel, layers, cols),
            out_shape=(pltpu.VMEM((3, 4, fb, rhs), f32), pltpu.VMEM((1, rhs), f32)),
            in_specs=[pl.BlockSpec(memory_space=pltpu.SMEM), vmem] + [hbm] * 6,
            out_specs=(vmem, vmem),
            scratch_shapes=[
                vec,
                vec,
                vec,
                mat,
                mat,
                pltpu.VMEM((2, nco), f32),
                wide,
                wide,
                vec,
                vec,
                pltpu.VMEM((3, 4, fb, rhs), f32),
                pltpu.VMEM((3, 4, fb, rhs), f32),
                pltpu.VMEM((2, rhs), f32),
                pltpu.VMEM((layers, 2, rhs), f32),
                pltpu.VMEM((2, n_late, 2, rhs), f32),
                pltpu.VMEM((layers, 2, nco), f32),
                pltpu.VMEM((128, nco), f32),
                pltpu.VMEM((nco, 128), f32),
                pltpu.VMEM((nco, 128), f32),
                pltpu.VMEM((cols // 2, 2, 2 * (layers - n_late), rhs), f32),
                pltpu.VMEM((cols // 2, 2, 2 * n_late, rhs), f32),
                pltpu.VMEM((16, rhs), f32),
                pltpu.VMEM((layers, 16, rhs), f32),
                pltpu.VMEM((layers, 4, rhs), f32),
                pltpu.VMEM((4, rhs), f32),
                pltpu.VMEM((128, rhs), f32),
                pltpu.VMEM((4, rhs), f32),
                pltpu.VMEM((cols, 4, rhs), f32),
                pltpu.VMEM((4, rhs), f32),
                pltpu.VMEM((4, rhs), f32),
                pltpu.SemaphoreType.DMA((9,)),
                pltpu.SemaphoreType.DMA((11,)),
                pltpu.SemaphoreType.DMA((11,)),
                pltpu.SemaphoreType.DMA((3,)),
                pltpu.SemaphoreType.DMA((3,)),
            ],
            compiler_params=pltpu.CompilerParams(
                collective_id=0, has_side_effects=True, vmem_limit_bytes=VMEM_LIMIT
            ),
        )(
            face_included.reshape(4),
            previous_rz.reshape(1, rhs),
            x,
            residual_in.reshape(4, fb, rhs),
            q,
            local_schur.reshape(nb, nb),
            local_inverse.reshape(nb, nb),
            coarse_inverse,
        )
        xo, ro, do, rz = pl.pallas_call(
            spread,
            out_shape=(field, field, field, scalar),
            in_specs=[vmem] * 2,
            out_specs=(hbm, hbm, hbm, hbm),
            scratch_shapes=[pltpu.SemaphoreType.DMA((4,))],
            compiler_params=pltpu.CompilerParams(vmem_limit_bytes=1024 * 1024),
        )(pltpu.with_memory_space_constraint(every, pltpu.VMEM), pltpu.with_memory_space_constraint(rz, pltpu.VMEM))
        shape = iterate.shape
        return xo.reshape(shape), ro.reshape(shape), do.reshape(shape), rz.reshape(rhs)

    placed = (
        P("layer", "col", None, None, None),
        P("layer", "col", None, None, None),
        P("layer", "col", None, None, None),
        P(),
        P("layer", "col", None, None),
        P("layer", "col", None, None),
        P(("layer", "col"), None),
        P("layer", "col", None),
    )
    return jax.shard_map(
        per_device,
        mesh=mesh,
        in_specs=placed,
        out_specs=(
            P("layer", "col", None, None, None),
            P("layer", "col", None, None, None),
            P("layer", "col", None, None, None),
            P(),
        ),
        check_vma=False,
    )
```
